32 devices in a mesh: grp: 2 (over y), dp: 4 (over x, core), tp: 4 (over z).
Axes of the slice: x: 2, y: 2, z: 4, core: 2. Of those that a mesh axis runs over, the one named last changes fastest.
Arguments:
- latents: bfloat16 [1024, 3072], P(('grp', 'dp', 'tp')), parts along dimension 0, may hold values from -6 to 6
- step_index: int32 [16], P(('grp', 'dp')), parts along dimension 0, may hold values from 0 to 2
- mod_table: float32 [4, 3, 3072], replicated, may hold values from -4 to 4
- base_up: bfloat16 [3072, 12288], P(None, 'tp'), may hold values from -0.109375 to 0.109375
- base_down: bfloat16 [12288, 3072], P('tp'), may hold values from -0.0546875 to 0.0546875
- up_a: bfloat16 [3072, 64], P(('dp', 'tp')), may hold values from -0.109375 to 0.109375
- up_b: bfloat16 [64, 12288], P('dp', 'tp'), may hold values from -0.75 to 0.75
- down_a: bfloat16 [12288, 64], P('tp', 'dp'), may hold values from -0.0546875 to 0.0546875
- down_b: bfloat16 [64, 3072], P(None, ('dp', 'tp')), may hold values from -0.75 to 0.75
Outputs:
- velocities: float32 [2, 1024, 3072], P(None, ('grp', 'dp', 'tp')), parts along dimension 1
- final_state: float32 [1024, 3072], P(('grp', 'dp', 'tp')), parts along dimension 0
The draws below stay inside these ranges and needn't reach their ends.
There are 2 independent parts, one for each index of `grp`. The reference program is written for one: setup_inputs(seed, part) draws one part's arguments, and reference() takes and returns one part's arrays. A program takes and returns all parts, laid end to end along the dimension named above; an argument that names none is the same for every part. Nothing has to cross between parts.
Inputs may be any that keep to these rules, and one draw needn't show every extreme that they name: `step_index`: the second step of an image uses the next index of the plan.
All inputs are finite; a program needn't handle non-finite values.
Results may differ from the reference program's by a relative error of at most 0.0061.
Values may be sent and summed in bfloat16 or wider, within the bound.
No kernel may reach another device: no remote copies, remote signals or barrier semaphores. Data moves between devices by JAX's collectives and lax.ppermute only.
A program may use at most 192 MiB of HBM per device.

```python
import jax
import jax.numpy as jnp
from jax import lax

D = 3072
FF = 12288
R = 64
NSTEPS = 4
IMG_ROWS = 64
TOKENS = 512
IMAGES = 8


def set_ends(array, key, smallest, largest):
    dims = array.shape
    spot = [jax.random.randint(jax.random.fold_in(key, axis), (), 0, dims[axis]) for axis in range(len(dims))]
    array = array.at[tuple(spot)].set(smallest)
    longest = dims.index(max(dims))
    spot[longest] = (spot[longest] + 1) % dims[longest]
    return array.at[tuple(spot)].set(largest)


def block_levels(key, extent, split, low, high):
    gain = 1.0
    for position, blocks in split:
        heights = jax.random.uniform(jax.random.fold_in(jax.random.fold_in(key, 6), position), (blocks,), jnp.float32, low / len(split), high / len(split))
        gain = gain * jnp.repeat(jnp.exp(heights), extent[position] // blocks).reshape((-1,) + (1,) * (len(extent) - 1 - position))
    return gain


def scatter_about(stream_key, dims, scale, bound, shards=(), held_as=jnp.bfloat16):
    gain = block_levels(stream_key, dims, shards, -0.22, 0.18) if shards else 1.0
    drawn = jax.random.normal(stream_key, dims, jnp.float32) * scale * gain
    return jnp.minimum(jnp.maximum(drawn, -bound), bound).astype(held_as)


def setup_inputs(seed: int = 0, part: int = 0) -> dict:
    key_list = jax.random.split(jax.random.key(seed), 10)
    part_keys = jax.random.split(jax.random.fold_in(key_list[9], part), 10)
    latents = scatter_about(part_keys[0], (TOKENS, D), 1.0, 6.0, ((0, 16),))
    step_index = set_ends(jax.random.randint(part_keys[1], (IMAGES,), 0, NSTEPS - 1), jax.random.fold_in(part_keys[1], 1), 0, (NSTEPS - 1) - 1).astype(jnp.int32)
    mod_table = scatter_about(key_list[2], (NSTEPS, 3, D), 0.8, 4.0, (), jnp.float32)
    base_up = scatter_about(key_list[3], (D, FF), D ** -0.5, 0.109375, ((1, 4),))
    base_down = scatter_about(key_list[4], (FF, D), FF ** -0.5, 0.0546875, ((0, 4),))
    up_a = scatter_about(key_list[5], (D, R), D ** -0.5, 0.109375, ((0, 16),))
    up_b = scatter_about(key_list[6], (R, FF), R ** -0.5, 0.75, ((0, 4), (1, 4)))
    down_a = scatter_about(key_list[7], (FF, R), FF ** -0.5, 0.0546875, ((0, 4), (1, 4)))
    down_b = scatter_about(key_list[8], (R, D), R ** -0.5, 0.75, ((1, 16),))
    return dict(latents=latents, step_index=step_index, mod_table=mod_table, base_up=base_up, base_down=base_down, up_a=up_a, up_b=up_b, down_a=down_a, down_b=down_b)


def normalize(state, shift, scale):
    mean = lax.optimization_barrier(jnp.mean(state, axis=1, keepdims=True))
    centered = state - mean
    spread = lax.optimization_barrier(jnp.mean(centered * centered, axis=1, keepdims=True))
    return (centered * lax.rsqrt(spread + 1e-06) * (1.0 + scale) + shift).astype(jnp.bfloat16)

def reference(latents, step_index, mod_table, base_up, base_down, up_a, up_b, down_a, down_b):
    merged_up = (base_up.astype(jnp.float32) + jnp.dot(up_a, up_b, preferred_element_type=jnp.float32)).astype(jnp.bfloat16)
    merged_down = (base_down.astype(jnp.float32) + jnp.dot(down_a, down_b, preferred_element_type=jnp.float32)).astype(jnp.bfloat16)
    state = latents.astype(jnp.float32)
    step_size = -1.0 / NSTEPS
    row_image = (jnp.arange(TOKENS) // IMG_ROWS).astype(jnp.int32)
    found = []
    for section in range(2):
        steps = step_index[row_image] + section
        mods = mod_table[steps]
        normed = normalize(state, mods[:, 0, :], mods[:, 1, :])
        upper = jnp.dot(normed, merged_up, preferred_element_type=jnp.float32)
        hidden = jax.nn.gelu(upper, approximate=True).astype(jnp.bfloat16)
        velocity = mods[:, 2, :] * jnp.dot(hidden, merged_down, preferred_element_type=jnp.float32)
        found.append(velocity)
        state = state + step_size * velocity
    return (jnp.stack(found), state)
```

```python
import functools

import jax
import jax.numpy as jnp
from jax import lax
from jax.experimental import pallas as pl
from jax.experimental.pallas import tpu as pltpu
from jax.sharding import PartitionSpec as P

NSTEPS = 4
STEP_SIZE = -1.0 / NSTEPS
BF16, F32 = jnp.bfloat16, jnp.float32
VMEM_GRANT = 16 << 20
VMEM = pl.BlockSpec(memory_space=pltpu.VMEM)
SMEM = pl.BlockSpec(memory_space=pltpu.SMEM)
HBM = pl.BlockSpec(memory_space=pltpu.HBM)
NT = (((1,), (1,)), ((), ()))


def call(body, outs, in_specs, out_specs, name, scratch=(), flops=0, bytes_accessed=0):
    return pl.pallas_call(
        body,
        out_shape=outs,
        in_specs=in_specs,
        out_specs=out_specs,
        scratch_shapes=list(scratch),
        compiler_params=pltpu.CompilerParams(vmem_limit_bytes=VMEM_GRANT),
        cost_estimate=pl.CostEstimate(
            flops=flops, bytes_accessed=bytes_accessed, transcendentals=0
        ),
        name=name,
    )


def shape(dims, dtype=BF16):
    return jax.ShapeDtypeStruct(dims, dtype)


def modulated(state, shift, scale):
    mean = jnp.mean(state, axis=1, keepdims=True)
    centered = state - mean
    spread = jnp.mean(centered * centered, axis=1, keepdims=True)
    return (centered * lax.rsqrt(spread + 1e-06) * (1.0 + scale) + shift).astype(BF16)


def gelu(x):
    return x * (0.5 * (1.0 + jnp.tanh(0.7978845608028654 * (x + 0.044715 * (x * x * x)))))


def mod_row(mod_ref, which, step):
    return mod_ref[which, pl.ds(step, 1), :]


def pack_body(slots, rank, ua_ref, db_ref, ub_ref, da_ref, p_ref, q_ref):
    rows = []
    for slot in range(slots):
        part = pl.ds(slot * rank, rank)
        rows += [ua_ref[part, :], db_ref[part, :]]
    both = jnp.concatenate(rows, axis=0).astype(F32)
    width = both.shape[0]
    eye = (
        lax.broadcasted_iota(jnp.int32, (width, width), 0)
        == lax.broadcasted_iota(jnp.int32, (width, width), 1)
    ).astype(F32)
    cols = lax.dot_general(
        both.astype(BF16), eye.astype(BF16), (((0,), (0,)), ((), ())), preferred_element_type=F32
    ).astype(BF16)
    height = p_ref.shape[0]
    for piece in range(cols.shape[0] // height):
        p_ref[:, piece * width : (piece + 1) * width] = cols[piece * height : (piece + 1) * height, :]
    q_ref[0:rank, :] = ub_ref[...]
    q_ref[rank : 2 * rank, :] = da_ref[...]


def norm_body(steps_ref, place_ref, lat_ref, mod_ref, out_ref):
    step = steps_ref[place_ref[2]]
    state = lat_ref[...].astype(F32)
    out_ref[...] = modulated(state, mod_row(mod_ref, 0, step), mod_row(mod_ref, 1, step))


def fetch_body(parts, src_ref, dst_ref, sems):
    rows = src_ref.shape[0] // parts
    copies = [
        pltpu.make_async_copy(
            src_ref.at[pl.ds(i * rows, rows)], dst_ref.at[pl.ds(i * rows, rows)], sems.at[i]
        )
        for i in range(parts)
    ]
    for copy in copies:
        copy.start()
    for copy in copies:
        copy.wait()


def fetch(src, name):
    parts = 8
    return call(
        functools.partial(fetch_body, parts),
        pltpu.VMEM(src.shape, src.dtype),
        [HBM],
        VMEM,
        name,
        [pltpu.SemaphoreType.DMA((parts,))],
        bytes_accessed=2 * src.size * src.dtype.itemsize,
    )(src)


def assemble_body(tp, dp, place_ref, *refs):
    p_parts, q_parts, (p_ref, q_ref) = refs[:dp], refs[dp : 2 * dp], refs[2 * dp :]
    me_tp, me_dp = place_ref[0], place_ref[1]
    height = q_parts[0].shape[0]
    width = p_ref.shape[1]
    per_block = p_ref.shape[0] // (tp * dp)
    pieces = per_block // height
    for j in range(dp):
        owner = me_dp ^ j
        q_ref[pl.ds(pl.multiple_of(owner * height, height), height), :] = q_parts[j][...]
        for k in range(tp):
            base = (owner * tp + (me_tp ^ k)) * per_block
            for piece in range(pieces):
                col = (k * pieces + piece) * width
                p_ref[pl.ds(pl.multiple_of(base + piece * height, height), height), :] = p_parts[j][
                    :, col : col + width
                ]


def ffn_body(tp, rank, tile, *refs):
    x_refs, (wu_ref, wd_ref, p_ref, q_ref), rest = refs[:tp], refs[tp : tp + 4], refs[tp + 4 :]
    own_ref, send_refs, (x_all, hidden) = rest[0], rest[1:tp], rest[tp:]
    count = x_refs[0].shape[0]
    for k in range(tp):
        x_all[k * count : (k + 1) * count, :] = x_refs[k][...]
    lanes = lax.broadcasted_iota(jnp.int32, (1, p_ref.shape[1]), 1)
    first_half = (lanes // rank) % 2 == 0
    low = jnp.dot(x_all[...], p_ref[...], preferred_element_type=F32)
    low = jnp.where(first_half, low, 0.0).astype(BF16)
    for i in range(hidden.shape[1] // tile):
        cols = slice(i * tile, (i + 1) * tile)
        upper = jnp.dot(x_all[...], wu_ref[:, cols], preferred_element_type=F32)
        upper += jnp.dot(low, q_ref[:, cols], preferred_element_type=F32)
        hidden[:, cols] = gelu(upper).astype(BF16)
    low = lax.dot_general(hidden[...], q_ref[...], NT, preferred_element_type=F32)
    low = jnp.where(first_half, 0.0, low).astype(BF16)
    for i in range(x_all.shape[1] // tile):
        cols = slice(i * tile, (i + 1) * tile)
        out = jnp.dot(hidden[...], wd_ref[:, cols], preferred_element_type=F32)
        out += lax.dot_general(low, p_ref[cols, :], NT, preferred_element_type=F32)
        own_ref[:, cols] = out[:count]
        for k in range(1, tp):
            send_refs[k - 1][:, cols] = out[k * count : (k + 1) * count].astype(BF16)


def middle_body(tp, steps_ref, place_ref, lat_ref, mod_ref, *refs):
    parts, (vel_ref, state_ref, out_ref) = refs[:tp], refs[tp:]
    step = steps_ref[place_ref[2]]
    total = parts[0][...]
    for part in parts[1:]:
        total += part[...].astype(F32)
    vel = mod_row(mod_ref, 2, step) * total
    state = lat_ref[...].astype(F32) + STEP_SIZE * vel
    vel_ref[...] = vel
    state_ref[...] = state
    out_ref[...] = modulated(state, mod_row(mod_ref, 0, step + 1), mod_row(mod_ref, 1, step + 1))


def last_body(tp, steps_ref, place_ref, state_ref, mod_ref, vel_ref, *refs):
    parts, (vels_ref, out_ref) = refs[:tp], refs[tp:]
    step = steps_ref[place_ref[2]] + 1
    total = parts[0][...]
    for part in parts[1:]:
        total += part[...].astype(F32)
    vel = mod_row(mod_ref, 2, step) * total
    vels_ref[0] = vel_ref[...]
    vels_ref[1] = vel
    out_ref[...] = state_ref[...] + STEP_SIZE * vel


def swap(x, axis, flip):
    return lax.ppermute(x, axis, [(i, i ^ flip) for i in range(lax.axis_size(axis))])


def fast(latents, step_index, mod_table, base_up, base_down, up_a, up_b, down_a, down_b):
    tp, dp = lax.axis_size("tp"), lax.axis_size("dp")
    count, width = latents.shape
    hidden = base_up.shape[1]
    rank = up_b.shape[0]
    both = 2 * rank * dp
    height = 2 * rank
    image_rows = count * tp // step_index.shape[0]
    me_tp, me_dp = lax.axis_index("tp"), lax.axis_index("dp")
    place = jnp.stack([me_tp, me_dp, me_tp * count // image_rows]).astype(jnp.int32)
    mods = jnp.transpose(mod_table, (1, 0, 2))

    p_own, q_own = call(
        functools.partial(pack_body, dp, rank),
        (shape((height, up_a.shape[0] // height * both)), shape((height, hidden))),
        [VMEM] * 4,
        (VMEM, VMEM),
        "pack_factors",
    )(up_a.T, down_b, up_b, down_a.T)
    normed = call(
        norm_body, shape((count, width)), [SMEM, SMEM, VMEM, VMEM], VMEM, "first_norm"
    )(step_index, place, latents, mods)

    p_line = [p_own] + [swap(p_own, "tp", k) for k in range(1, tp)]
    x_parts = [normed] + [swap(normed, "tp", k) for k in range(1, tp)]
    q_far = swap(q_own, "dp", 2)
    merged_up = fetch(base_up, "fetch_up")
    p_line = jnp.concatenate(p_line, axis=1)
    p_far = swap(p_line, "dp", 2)
    merged_down = fetch(base_down, "fetch_down")
    near = [swap(a, "dp", 1) for a in (p_line, q_own, p_far, q_far)]
    p_all, q_all = call(
        functools.partial(assemble_body, tp, dp),
        (shape((width, both)), shape((both, hidden))),
        [SMEM] + [VMEM] * (2 * dp),
        (VMEM, VMEM),
        "assemble_factors",
    )(place, p_line, near[0], p_far, near[2], q_own, near[1], q_far, near[3])

    wu = pltpu.with_memory_space_constraint(merged_up, pltpu.VMEM)
    wd = pltpu.with_memory_space_constraint(merged_down, pltpu.VMEM)

    def block(parts, name):
        rows = count * tp
        return call(
            functools.partial(ffn_body, tp, rank, 1024),
            (shape((count, width), F32),) + (shape((count, width)),) * (tp - 1),
            [VMEM] * (tp + 4),
            (VMEM,) * tp,
            name,
            [pltpu.VMEM((rows, width), BF16), pltpu.VMEM((rows, hidden), BF16)],
            flops=4 * rows * width * hidden,
            bytes_accessed=4 * width * hidden,
        )(*parts, wu, wd, p_all, q_all)

    def exchange(parts):
        return [parts[0]] + [swap(part, "tp", k) for k, part in enumerate(parts[1:], 1)]

    sums = exchange(block(x_parts, "block_first"))
    vel, state, normed = call(
        functools.partial(middle_body, tp),
        (shape((count, width), F32), shape((count, width), F32), shape((count, width))),
        [SMEM, SMEM] + [VMEM] * (2 + tp),
        (VMEM,) * 3,
        "first_update",
    )(step_index, place, latents, mods, *sums)
    x_parts = [normed] + [swap(normed, "tp", k) for k in range(1, tp)]
    sums = exchange(block(x_parts, "block_second"))
    return call(
        functools.partial(last_body, tp),
        (shape((2, count, width), F32), shape((count, width), F32)),
        [SMEM, SMEM] + [VMEM] * (3 + tp),
        (VMEM,) * 2,
        "second_update",
    )(step_index, place, state, mods, vel, *sums)


def normalize(state, shift, scale):
    mean = jnp.mean(state, axis=1, keepdims=True)
    centered = state - mean
    spread = jnp.mean(centered * centered, axis=1, keepdims=True)
    return (centered * lax.rsqrt(spread + 1e-06) * (1.0 + scale) + shift).astype(jnp.bfloat16)


def plain(latents, step_index, mod_table, base_up, base_down, up_a, up_b, down_a, down_b):
    full_up_a, full_down_b = (
        lax.all_gather(up_a, ("dp", "tp"), axis=0, tiled=True),
        lax.all_gather(down_b, ("dp", "tp"), axis=1, tiled=True),
    )
    cols_up_b, rows_down_a = (
        lax.all_gather(up_b, "dp", axis=0, tiled=True),
        lax.all_gather(down_a, "dp", axis=1, tiled=True),
    )
    merged_up = (
        base_up.astype(jnp.float32)
        + jnp.dot(full_up_a, cols_up_b, preferred_element_type=jnp.float32)
    ).astype(jnp.bfloat16)
    merged_down = (
        base_down.astype(jnp.float32)
        + jnp.dot(rows_down_a, full_down_b, preferred_element_type=jnp.float32)
    ).astype(jnp.bfloat16)
    own_count = latents.shape[0]
    group_rows = own_count * lax.axis_size("tp")
    image_count = step_index.shape[0]
    image_rows = group_rows // image_count
    own_start = lax.axis_index("tp") * own_count
    step_size = -1.0 / NSTEPS

    def row_steps(count, offset):
        rows = jnp.arange(count, dtype=jnp.int32)
        image = rows // image_rows
        picks = (image[:, None] == jnp.arange(image_count, dtype=jnp.int32)[None, :]).astype(
            jnp.int32
        )
        return jnp.sum(picks * step_index[None, :], axis=1) + offset

    def modulation(steps):
        onehot = (steps[:, None] == jnp.arange(NSTEPS, dtype=jnp.int32)[None, :]).astype(
            jnp.float32
        )
        shift = jnp.dot(onehot, mod_table[:, 0, :], precision=lax.Precision.HIGHEST)
        scale = jnp.dot(onehot, mod_table[:, 1, :], precision=lax.Precision.HIGHEST)
        gate = jnp.dot(onehot, mod_table[:, 2, :], precision=lax.Precision.HIGHEST)
        return (shift, scale, gate)

    def project(normed):
        upper = jnp.dot(normed, merged_up, preferred_element_type=jnp.float32)
        hidden = jax.nn.gelu(upper, approximate=True).astype(jnp.bfloat16)
        return jnp.dot(hidden, merged_down, preferred_element_type=jnp.float32)

    state_all = lax.all_gather(latents, "tp", axis=0, tiled=True).astype(jnp.float32)
    shift, scale, gate = modulation(row_steps(group_rows, 0))
    normed = normalize(state_all, shift, scale)
    first = gate * lax.psum(project(normed), "tp")
    state_all = state_all + step_size * first
    shift, scale, gate = modulation(row_steps(group_rows, 1))
    normed = normalize(state_all, shift, scale)
    gate_own = lax.dynamic_slice_in_dim(gate, own_start, own_count, 0)
    second = gate_own * lax.psum_scatter(project(normed), "tp", scatter_dimension=0, tiled=True)
    state_own = lax.dynamic_slice_in_dim(state_all, own_start, own_count, 0) + step_size * second
    first_own = lax.dynamic_slice_in_dim(first, own_start, own_count, 0)
    return (jnp.stack([first_own, second]), state_own)


def solution(mesh):
    tp, dp = mesh.shape["tp"], mesh.shape["dp"]

    def local(*args):
        latents, step_index, mod_table, base_up, base_down, up_a, up_b = args[:7]
        whole_tiles = (
            tp == 4
            and dp == 4
            and latents.shape[0] % 16 == 0
            and base_up.shape[1] % 1024 == 0
            and base_up.shape[0] % 1024 == 0
            and up_b.shape[0] % 16 == 0
            and up_a.shape[0] % (2 * up_b.shape[0]) == 0
            and (latents.shape[0] * tp // step_index.shape[0]) % latents.shape[0] == 0
        )
        return (fast if whole_tiles else plain)(*args)

    return jax.shard_map(
        local,
        mesh=mesh,
        in_specs=(
            P(("grp", "dp", "tp"), None),
            P(("grp", "dp")),
            P(),
            P(None, "tp"),
            P("tp", None),
            P(("dp", "tp"), None),
            P("dp", "tp"),
            P("tp", "dp"),
            P(None, ("dp", "tp")),
        ),
        out_specs=(P(None, ("grp", "dp", "tp"), None), P(("grp", "dp", "tp"), None)),
        check_vma=False,
    )
```

```python
import functools

import jax
import jax.numpy as jnp
from jax import lax
from jax.experimental import pallas as pl
from jax.experimental.pallas import tpu as pltpu
from jax.sharding import PartitionSpec as P

NSTEPS = 4
STEP_SIZE = -1.0 / NSTEPS
BF16, F32 = jnp.bfloat16, jnp.float32
VMEM_GRANT = 4 << 20
VMEM = pl.BlockSpec(memory_space=pltpu.VMEM)
SMEM = pl.BlockSpec(memory_space=pltpu.SMEM)
HBM = pl.BlockSpec(memory_space=pltpu.HBM)
NT = (((1,), (1,)), ((), ()))


def call(body, outs, in_specs, out_specs, name, scratch=(), flops=0, bytes_accessed=0):
    return pl.pallas_call(
        body,
        out_shape=outs,
        in_specs=in_specs,
        out_specs=out_specs,
        scratch_shapes=list(scratch),
        compiler_params=pltpu.CompilerParams(vmem_limit_bytes=VMEM_GRANT),
        cost_estimate=pl.CostEstimate(
            flops=flops, bytes_accessed=bytes_accessed, transcendentals=0
        ),
        name=name,
    )


def shape(dims, dtype=BF16):
    return jax.ShapeDtypeStruct(dims, dtype)


def modulated(state, shift, scale):
    mean = jnp.mean(state, axis=1, keepdims=True)
    centered = state - mean
    spread = jnp.mean(centered * centered, axis=1, keepdims=True)
    return (centered * lax.rsqrt(spread + 1e-06) * (1.0 + scale) + shift).astype(BF16)


def gelu(x):
    return x * (0.5 * (1.0 + jnp.tanh(0.7978845608028654 * (x + 0.044715 * (x * x * x)))))


def mod_row(mod_ref, which, step):
    return mod_ref[which, pl.ds(step, 1), :]


def pack_body(slots, rank, ua_ref, db_ref, ub_ref, da_ref, p_ref, q_ref):
    rows = []
    for slot in range(slots):
        part = pl.ds(slot * rank, rank)
        rows += [ua_ref[part, :], db_ref[part, :]]
    both = jnp.concatenate(rows, axis=0).astype(F32)
    width = both.shape[0]
    eye = (
        lax.broadcasted_iota(jnp.int32, (width, width), 0)
        == lax.broadcasted_iota(jnp.int32, (width, width), 1)
    ).astype(F32)
    cols = lax.dot_general(
        both.astype(BF16), eye.astype(BF16), (((0,), (0,)), ((), ())), preferred_element_type=F32
    ).astype(BF16)
    height = p_ref.shape[0]
    for piece in range(cols.shape[0] // height):
        p_ref[:, piece * width : (piece + 1) * width] = cols[piece * height : (piece + 1) * height, :]
    q_ref[0:rank, :] = ub_ref[...]
    q_ref[rank : 2 * rank, :] = da_ref[...]


def norm_body(steps_ref, place_ref, lat_ref, mod_ref, out_ref):
    step = steps_ref[place_ref[2]]
    state = lat_ref[...].astype(F32)
    out_ref[...] = modulated(state, mod_row(mod_ref, 0, step), mod_row(mod_ref, 1, step))


def fetch_body(parts, src_ref, dst_ref, sems):
    rows = src_ref.shape[0] // parts
    copies = [
        pltpu.make_async_copy(
            src_ref.at[pl.ds(i * rows, rows)], dst_ref.at[pl.ds(i * rows, rows)], sems.at[i]
        )
        for i in range(parts)
    ]
    for copy in copies:
        copy.start()
    for copy in copies:
        copy.wait()


def fetch(src, name):
    parts = 8
    return call(
        functools.partial(fetch_body, parts),
        pltpu.VMEM(src.shape, src.dtype),
        [HBM],
        VMEM,
        name,
        [pltpu.SemaphoreType.DMA((parts,))],
        bytes_accessed=2 * src.size * src.dtype.itemsize,
    )(pltpu.with_memory_space_constraint(src, pltpu.HBM))


def assemble_body(tp, dp, place_ref, *refs):
    p_parts, q_parts, (p_ref, q_ref) = refs[:dp], refs[dp : 2 * dp], refs[2 * dp :]
    me_tp, me_dp = place_ref[0], place_ref[1]
    height = q_parts[0].shape[0]
    width = p_ref.shape[1]
    per_block = p_ref.shape[0] // (tp * dp)
    pieces = per_block // height
    for j in range(dp):
        owner = me_dp ^ j
        q_ref[pl.ds(pl.multiple_of(owner * height, height), height), :] = q_parts[j][...]
        for k in range(tp):
            base = (owner * tp + (me_tp ^ k)) * per_block
            for piece in range(pieces):
                col = (k * pieces + piece) * width
                p_ref[pl.ds(pl.multiple_of(base + piece * height, height), height), :] = p_parts[j][
                    :, col : col + width
                ]


def ffn_body(tp, rank, tile, *refs):
    x_refs, (wu_ref, wd_ref, p_ref, q_ref), rest = refs[:tp], refs[tp : tp + 4], refs[tp + 4 :]
    own_ref, send_refs, (x_all, hidden) = rest[0], rest[1:tp], rest[tp:]
    count = x_refs[0].shape[0]
    for k in range(tp):
        x_all[k * count : (k + 1) * count, :] = x_refs[k][...]
    lanes = lax.broadcasted_iota(jnp.int32, (1, p_ref.shape[1]), 1)
    first_half = (lanes // rank) % 2 == 0
    low = jnp.dot(x_all[...], p_ref[...], preferred_element_type=F32)
    low = jnp.where(first_half, low, 0.0).astype(BF16)
    for i in range(hidden.shape[1] // tile):
        cols = slice(i * tile, (i + 1) * tile)
        upper = jnp.dot(x_all[...], wu_ref[:, cols], preferred_element_type=F32)
        upper += jnp.dot(low, q_ref[:, cols], preferred_element_type=F32)
        hidden[:, cols] = gelu(upper).astype(BF16)
    low = lax.dot_general(hidden[...], q_ref[...], NT, preferred_element_type=F32)
    low = jnp.where(first_half, 0.0, low).astype(BF16)
    for i in range(x_all.shape[1] // tile):
        cols = slice(i * tile, (i + 1) * tile)
        out = jnp.dot(hidden[...], wd_ref[:, cols], preferred_element_type=F32)
        out += lax.dot_general(low, p_ref[cols, :], NT, preferred_element_type=F32)
        own_ref[:, cols] = out[:count]
        for k in range(1, tp):
            send_refs[k - 1][:, cols] = out[k * count : (k + 1) * count].astype(BF16)


def middle_body(tp, steps_ref, place_ref, lat_ref, mod_ref, *refs):
    parts, (vel_ref, state_ref, out_ref) = refs[:tp], refs[tp:]
    step = steps_ref[place_ref[2]]
    total = parts[0][...]
    for part in parts[1:]:
        total += part[...].astype(F32)
    vel = mod_row(mod_ref, 2, step) * total
    state = lat_ref[...].astype(F32) + STEP_SIZE * vel
    vel_ref[...] = vel
    state_ref[...] = state
    out_ref[...] = modulated(state, mod_row(mod_ref, 0, step + 1), mod_row(mod_ref, 1, step + 1))


def last_body(tp, steps_ref, place_ref, state_ref, mod_ref, vel_ref, *refs):
    parts, (vels_ref, out_ref) = refs[:tp], refs[tp:]
    step = steps_ref[place_ref[2]] + 1
    total = parts[0][...]
    for part in parts[1:]:
        total += part[...].astype(F32)
    vel = mod_row(mod_ref, 2, step) * total
    vels_ref[0] = vel_ref[...]
    vels_ref[1] = vel
    out_ref[...] = state_ref[...] + STEP_SIZE * vel


def swap(x, axis, flip):
    return lax.ppermute(x, axis, [(i, i ^ flip) for i in range(lax.axis_size(axis))])


def fast(latents, step_index, mod_table, base_up, base_down, up_a, up_b, down_a, down_b):
    tp, dp = lax.axis_size("tp"), lax.axis_size("dp")
    count, width = latents.shape
    hidden = base_up.shape[1]
    rank = up_b.shape[0]
    both = 2 * rank * dp
    height = 2 * rank
    image_rows = count * tp // step_index.shape[0]
    me_tp, me_dp = lax.axis_index("tp"), lax.axis_index("dp")
    place = jnp.stack([me_tp, me_dp, me_tp * count // image_rows]).astype(jnp.int32)
    mods = jnp.transpose(mod_table, (1, 0, 2))

    p_own, q_own = call(
        functools.partial(pack_body, dp, rank),
        (shape((height, up_a.shape[0] // height * both)), shape((height, hidden))),
        [VMEM] * 4,
        (VMEM, VMEM),
        "pack_factors",
    )(up_a.T, down_b, up_b, down_a.T)
    normed = call(
        norm_body, shape((count, width)), [SMEM, SMEM, VMEM, VMEM], VMEM, "first_norm"
    )(step_index, place, latents, mods)

    p_line = [p_own] + [swap(p_own, "tp", k) for k in range(1, tp)]
    x_parts = [normed] + [swap(normed, "tp", k) for k in range(1, tp)]
    q_far = swap(q_own, "dp", 2)
    merged_up = fetch(base_up, "fetch_up")
    p_line = jnp.concatenate(p_line, axis=1)
    p_far = swap(p_line, "dp", 2)
    merged_down = fetch(base_down, "fetch_down")
    near = [swap(a, "dp", 1) for a in (p_line, q_own, p_far, q_far)]
    p_all, q_all = call(
        functools.partial(assemble_body, tp, dp),
        (pltpu.VMEM((width, both), BF16), pltpu.VMEM((both, hidden), BF16)),
        [SMEM] + [VMEM] * (2 * dp),
        (VMEM, VMEM),
        "assemble_factors",
    )(place, p_line, near[0], p_far, near[2], q_own, near[1], q_far, near[3])

    wu = pltpu.with_memory_space_constraint(merged_up, pltpu.VMEM)
    wd = pltpu.with_memory_space_constraint(merged_down, pltpu.VMEM)
    p_all = pltpu.with_memory_space_constraint(p_all, pltpu.VMEM)
    q_all = pltpu.with_memory_space_constraint(q_all, pltpu.VMEM)

    def block(parts, name):
        rows = count * tp
        return call(
            functools.partial(ffn_body, tp, rank, 1024),
            (shape((count, width), F32),) + (shape((count, width)),) * (tp - 1),
            [VMEM] * (tp + 4),
            (VMEM,) * tp,
            name,
            [pltpu.VMEM((rows, width), BF16), pltpu.VMEM((rows, hidden), BF16)],
            flops=4 * rows * width * hidden,
            bytes_accessed=4 * width * hidden,
        )(*parts, wu, wd, p_all, q_all)

    def exchange(parts):
        return [parts[0]] + [swap(part, "tp", k) for k, part in enumerate(parts[1:], 1)]

    sums = exchange(block(x_parts, "block_first"))
    vel, state, normed = call(
        functools.partial(middle_body, tp),
        (shape((count, width), F32), shape((count, width), F32), shape((count, width))),
        [SMEM, SMEM] + [VMEM] * (2 + tp),
        (VMEM,) * 3,
        "first_update",
    )(step_index, place, latents, mods, *sums)
    x_parts = [normed] + [swap(normed, "tp", k) for k in range(1, tp)]
    sums = exchange(block(x_parts, "block_second"))
    return call(
        functools.partial(last_body, tp),
        (shape((2, count, width), F32), shape((count, width), F32)),
        [SMEM, SMEM] + [VMEM] * (3 + tp),
        (VMEM,) * 2,
        "second_update",
    )(step_index, place, state, mods, vel, *sums)


def normalize(state, shift, scale):
    mean = jnp.mean(state, axis=1, keepdims=True)
    centered = state - mean
    spread = jnp.mean(centered * centered, axis=1, keepdims=True)
    return (centered * lax.rsqrt(spread + 1e-06) * (1.0 + scale) + shift).astype(jnp.bfloat16)


def plain(latents, step_index, mod_table, base_up, base_down, up_a, up_b, down_a, down_b):
    full_up_a, full_down_b = (
        lax.all_gather(up_a, ("dp", "tp"), axis=0, tiled=True),
        lax.all_gather(down_b, ("dp", "tp"), axis=1, tiled=True),
    )
    cols_up_b, rows_down_a = (
        lax.all_gather(up_b, "dp", axis=0, tiled=True),
        lax.all_gather(down_a, "dp", axis=1, tiled=True),
    )
    merged_up = (
        base_up.astype(jnp.float32)
        + jnp.dot(full_up_a, cols_up_b, preferred_element_type=jnp.float32)
    ).astype(jnp.bfloat16)
    merged_down = (
        base_down.astype(jnp.float32)
        + jnp.dot(rows_down_a, full_down_b, preferred_element_type=jnp.float32)
    ).astype(jnp.bfloat16)
    own_count = latents.shape[0]
    group_rows = own_count * lax.axis_size("tp")
    image_count = step_index.shape[0]
    image_rows = group_rows // image_count
    own_start = lax.axis_index("tp") * own_count
    step_size = -1.0 / NSTEPS

    def row_steps(count, offset):
        rows = jnp.arange(count, dtype=jnp.int32)
        image = rows // image_rows
        picks = (image[:, None] == jnp.arange(image_count, dtype=jnp.int32)[None, :]).astype(
            jnp.int32
        )
        return jnp.sum(picks * step_index[None, :], axis=1) + offset

    def modulation(steps):
        onehot = (steps[:, None] == jnp.arange(NSTEPS, dtype=jnp.int32)[None, :]).astype(
            jnp.float32
        )
        shift = jnp.dot(onehot, mod_table[:, 0, :], precision=lax.Precision.HIGHEST)
        scale = jnp.dot(onehot, mod_table[:, 1, :], precision=lax.Precision.HIGHEST)
        gate = jnp.dot(onehot, mod_table[:, 2, :], precision=lax.Precision.HIGHEST)
        return (shift, scale, gate)

    def project(normed):
        upper = jnp.dot(normed, merged_up, preferred_element_type=jnp.float32)
        hidden = jax.nn.gelu(upper, approximate=True).astype(jnp.bfloat16)
        return jnp.dot(hidden, merged_down, preferred_element_type=jnp.float32)

    state_all = lax.all_gather(latents, "tp", axis=0, tiled=True).astype(jnp.float32)
    shift, scale, gate = modulation(row_steps(group_rows, 0))
    normed = normalize(state_all, shift, scale)
    first = gate * lax.psum(project(normed), "tp")
    state_all = state_all + step_size * first
    shift, scale, gate = modulation(row_steps(group_rows, 1))
    normed = normalize(state_all, shift, scale)
    gate_own = lax.dynamic_slice_in_dim(gate, own_start, own_count, 0)
    second = gate_own * lax.psum_scatter(project(normed), "tp", scatter_dimension=0, tiled=True)
    state_own = lax.dynamic_slice_in_dim(state_all, own_start, own_count, 0) + step_size * second
    first_own = lax.dynamic_slice_in_dim(first, own_start, own_count, 0)
    return (jnp.stack([first_own, second]), state_own)


def solution(mesh):
    tp, dp = mesh.shape["tp"], mesh.shape["dp"]

    def local(*args):
        latents, step_index, mod_table, base_up, base_down, up_a, up_b = args[:7]
        whole_tiles = (
            tp == 4
            and dp == 4
            and latents.shape[0] % 16 == 0
            and base_up.shape[1] % 1024 == 0
            and base_up.shape[0] % 1024 == 0
            and up_b.shape[0] % 16 == 0
            and up_a.shape[0] % (2 * up_b.shape[0]) == 0
            and (latents.shape[0] * tp // step_index.shape[0]) % latents.shape[0] == 0
        )
        return (fast if whole_tiles else plain)(*args)

    return jax.shard_map(
        local,
        mesh=mesh,
        in_specs=(
            P(("grp", "dp", "tp"), None),
            P(("grp", "dp")),
            P(),
            P(None, "tp"),
            P("tp", None),
            P(("dp", "tp"), None),
            P("dp", "tp"),
            P("tp", "dp"),
            P(None, ("dp", "tp")),
        ),
        out_specs=(P(None, ("grp", "dp", "tp"), None), P(("grp", "dp", "tp"), None)),
        check_vma=False,
    )
```

```python
import functools

import jax
import jax.numpy as jnp
from jax import lax
from jax.experimental import pallas as pl
from jax.experimental.pallas import tpu as pltpu
from jax.sharding import PartitionSpec as P

NSTEPS = 4
STREAMS = 4
TOKEN_ORDER = (1, 3, 2)
STEP_SIZE = -1.0 / NSTEPS
BF16, F32 = jnp.bfloat16, jnp.float32
VMEM_GRANT = 4 << 20
VMEM = pl.BlockSpec(memory_space=pltpu.VMEM)
SMEM = pl.BlockSpec(memory_space=pltpu.SMEM)
HBM = pl.BlockSpec(memory_space=pltpu.HBM)
NT = (((1,), (1,)), ((), ()))


def call(body, outs, in_specs, out_specs, name, scratch=(), flops=0, bytes_accessed=0):
    return pl.pallas_call(
        body,
        out_shape=outs,
        in_specs=in_specs,
        out_specs=out_specs,
        scratch_shapes=list(scratch),
        compiler_params=pltpu.CompilerParams(vmem_limit_bytes=VMEM_GRANT),
        cost_estimate=pl.CostEstimate(
            flops=flops, bytes_accessed=bytes_accessed, transcendentals=0
        ),
        name=name,
    )


def shape(dims, dtype=BF16):
    return jax.ShapeDtypeStruct(dims, dtype)


def modulated(state, shift, scale):
    mean = jnp.mean(state, axis=1, keepdims=True)
    centered = state - mean
    spread = jnp.mean(centered * centered, axis=1, keepdims=True)
    return (centered * lax.rsqrt(spread + 1e-06) * (1.0 + scale) + shift).astype(BF16)


def gelu(x):
    return x * (0.5 * (1.0 + jnp.tanh(0.7978845608028654 * (x + 0.044715 * (x * x * x)))))


def own_image(count, images):
    tp = lax.axis_size("tp")
    return lax.axis_index("tp") * images // tp


def mod_row(mod_ref, which, step):
    return mod_ref[which, pl.ds(step, 1), :]


def prepare_body(slots, rank, *refs):
    sources, outs, held, sems = refs[:7], refs[7:10], refs[10:17], refs[-1]
    copies = [
        pltpu.make_async_copy(src, dst, sems.at[i])
        for i, (src, dst) in enumerate(zip(sources, held))
    ]
    for copy in copies:
        copy.start()
    for copy in copies:
        copy.wait()
    ua_ref, db_ref, ub_ref, da_ref, steps_ref, lat_ref, mod_ref = held
    p_ref, q_ref = outs[:2]
    rows = []
    for slot in range(slots):
        part = pl.ds(slot * rank, rank)
        rows += [ua_ref[part, :], db_ref[part, :]]
    both = jnp.concatenate(rows, axis=0)
    width = both.shape[0]
    eye = (
        lax.broadcasted_iota(jnp.int32, (width, width), 0)
        == lax.broadcasted_iota(jnp.int32, (width, width), 1)
    ).astype(F32)
    cols = lax.dot_general(
        both, eye.astype(BF16), (((0,), (0,)), ((), ())), preferred_element_type=F32
    ).astype(BF16)
    height = p_ref.shape[0]
    for piece in range(cols.shape[0] // height):
        p_ref[:, piece * width : (piece + 1) * width] = cols[piece * height : (piece + 1) * height, :]
    q_ref[0:rank, :] = ub_ref[...]
    q_ref[rank : 2 * rank, :] = da_ref[...]
    step = steps_ref[own_image(lat_ref.shape[0], steps_ref.shape[0])]
    state = lat_ref[...].astype(F32)
    outs[2][...] = modulated(state, mod_row(mod_ref, 0, step), mod_row(mod_ref, 1, step))


def fetch_body(start, source, target, sems):
    copies = stream_copies(source, target, sems, start)
    for copy in copies:
        copy.start()
    for copy in copies:
        copy.wait()


def assemble_body(tp, dp, *refs):
    p_parts, q_parts, (p_ref, q_ref, pt_ref, qt_ref) = refs[:dp], refs[dp : 2 * dp], refs[2 * dp :]
    me_tp, me_dp = lax.axis_index("tp"), lax.axis_index("dp")
    height = q_parts[0].shape[0]
    width = p_ref.shape[1]
    per_block = p_ref.shape[0] // (tp * dp)
    pieces = per_block // height
    for j in range(dp):
        owner = me_dp ^ j
        q_ref[pl.ds(pl.multiple_of(owner * height, height), height), :] = q_parts[j][...]
        for k in range(tp):
            base = (owner * tp + (me_tp ^ k)) * per_block
            for piece in range(pieces):
                col = (k * pieces + piece) * width
                p_ref[pl.ds(pl.multiple_of(base + piece * height, height), height), :] = p_parts[j][
                    :, col : col + width
                ]
    pt_ref[...] = p_ref[...].T
    qt_ref[...] = q_ref[...].T


def stream_copies(source, target, sems, start):
    rows = target.shape[0] // STREAMS
    copies = []
    for i in range(STREAMS):
        block = pl.ds(i * rows, rows)
        copies.append(
            pltpu.make_async_copy(
                source.at[block, pl.ds(start, target.shape[1])], target.at[block], sems.at[i]
            )
        )
    return copies


def start_stream(source, target, sems, start):
    rows = target.shape[0] // STREAMS
    cols = pl.ds(start, target.shape[1])

    @pl.loop(0, STREAMS)
    def _(i):
        block = pl.ds(pl.multiple_of(i * rows, rows), rows)
        pltpu.make_async_copy(source.at[block, cols], target.at[block], sems.at[i]).start()


def block_body(streamed, rank, *refs):
    given = 4 if streamed else 6
    x_refs, refs = refs[:given], refs[given:]
    (p_ref, q_ref, pt_ref, qt_ref), wu_refs, refs = refs[:4], refs[4:6], refs[6:]
    if streamed:
        source, outs, wd_refs, (x_all, hidden, sems) = refs[0], refs[1:7], refs[7:9], refs[9:]
        for i, target in enumerate(wd_refs):
            start_stream(source, target, sems.at[i], i * target.shape[1])
    else:
        wd_refs, outs, (x_all, hidden) = refs[:2], refs[2:8], refs[8:]
    count, width = x_refs[0].shape
    half = width // 2
    if streamed:
        for k, x_ref in enumerate(x_refs):
            x_all[k * count : (k + 1) * count, :] = x_ref[...]
    else:
        own_ref, near_ref, far_ref, over_ref, rest_2_ref, rest_3_ref = x_refs
        x_all[:count, :] = own_ref[...]
        x_all[count : 2 * count, :] = near_ref[...]
        x_all[2 * count : 3 * count, :half] = far_ref[...]
        x_all[2 * count : 3 * count, half:] = rest_2_ref[...]
        x_all[3 * count :, :half] = over_ref[...]
        x_all[3 * count :, half:] = rest_3_ref[...]
    lanes = lax.broadcasted_iota(jnp.int32, (1, p_ref.shape[1]), 1)
    first_half = (lanes // rank) % 2 == 0
    low = jnp.dot(x_all[...], p_ref[...], preferred_element_type=F32)
    low = jnp.where(first_half, low, 0.0).astype(BF16)
    tile = wu_refs[0].shape[1]
    for i, wu_ref in enumerate(wu_refs):
        cols = slice(i * tile, (i + 1) * tile)
        upper = jnp.dot(x_all[...], wu_ref[...], preferred_element_type=F32)
        upper += jnp.dot(low, q_ref[:, cols], preferred_element_type=F32)
        hidden[:, cols] = gelu(upper).astype(BF16)
    low = jnp.dot(hidden[...], qt_ref[...], preferred_element_type=F32)
    low = jnp.where(first_half, 0.0, low).astype(BF16)
    own_out, near_out, over_out, far_out, rest_2_out, rest_3_out = outs
    for i, wd_ref in enumerate(wd_refs):
        cols = slice(i * half, (i + 1) * half)
        if streamed:
            for copy in stream_copies(source, wd_ref, sems.at[i], i * half):
                copy.wait()
        out = jnp.dot(hidden[...], wd_ref[...], preferred_element_type=F32)
        out += jnp.dot(low, pt_ref[:, cols], preferred_element_type=F32)
        own_out[:, cols] = out[:count]
        near_out[:, cols] = out[count : 2 * count].astype(BF16)
        if i == 0:
            far_out[...] = out[2 * count : 3 * count]
            over_out[...] = out[3 * count :].astype(BF16)
        else:
            rest_2_out[...] = out[2 * count : 3 * count].astype(BF16)
            rest_3_out[...] = out[3 * count :].astype(BF16)


def relay_body(mine_ref, got_ref, out_ref):
    out_ref[...] = (mine_ref[...] + got_ref[...].astype(F32)).astype(BF16)


def summed(own_ref, near_ref, far_ref, rest_2_ref, rest_3_ref):
    half = far_ref.shape[1]
    total = own_ref[...] + near_ref[...].astype(F32)
    first = total[:, :half] + far_ref[...].astype(F32)
    second = total[:, half:] + rest_2_ref[...].astype(F32) + rest_3_ref[...].astype(F32)
    return jnp.concatenate([first, second], axis=1)


def middle_body(steps_ref, lat_ref, mod_ref, *refs):
    parts, (vel_ref, state_ref, out_ref, far_ref, rest_ref) = refs[:5], refs[5:]
    step = steps_ref[own_image(lat_ref.shape[0], steps_ref.shape[0])]
    vel = mod_row(mod_ref, 2, step) * summed(*parts)
    state = lat_ref[...].astype(F32) + STEP_SIZE * vel
    vel_ref[...] = vel
    state_ref[...] = state
    normed = modulated(state, mod_row(mod_ref, 0, step + 1), mod_row(mod_ref, 1, step + 1))
    half = far_ref.shape[1]
    out_ref[...] = normed
    far_ref[...] = normed[:, :half]
    rest_ref[...] = normed[:, half:]


def last_body(steps_ref, mod_ref, vel_ref, state_ref, *refs):
    parts, (vels_ref, out_ref) = refs[:-2], refs[-2:]
    step = steps_ref[own_image(out_ref.shape[0], steps_ref.shape[0])] + 1
    vel = mod_row(mod_ref, 2, step) * summed(*parts)
    vels_ref[0] = vel_ref[...]
    vels_ref[1] = vel
    out_ref[...] = state_ref[...] + STEP_SIZE * vel


def swap(x, axis, flip):
    return lax.ppermute(x, axis, [(i, i ^ flip) for i in range(lax.axis_size(axis))])


def spread(whole, rest, far):
    return dict(
        over=swap(far, "tp", 1),
        near=swap(whole, "tp", 1),
        rest_2=swap(rest, "tp", 2),
        rest_3=swap(rest, "tp", 3),
    )


def gather(own, got, far):
    return [own, got["near"], far, got["over"], got["rest_2"], got["rest_3"]]


def reduce(own, near, over, far, rest_2, rest_3):
    count, half = far.shape
    relayed = call(relay_body, shape((count, half)), [VMEM] * 2, VMEM, "relay")(
        far, swap(over, "tp", 1)
    )
    return (
        own,
        swap(near, "tp", 1),
        swap(relayed, "tp", 2),
        swap(rest_2, "tp", 2),
        swap(rest_3, "tp", 3),
    )


def pinned(x, space):
    return pltpu.with_memory_space_constraint(x, space)


def fast(latents, step_index, mod_table, base_up, base_down, up_a, up_b, down_a, down_b):
    tp, dp = lax.axis_size("tp"), lax.axis_size("dp")
    count, width = latents.shape
    rows = count * tp
    half = width // 2
    hidden = base_up.shape[1]
    rank = up_b.shape[0]
    both = 2 * rank * dp
    height = 2 * rank
    extra = up_a.shape[0] // height * both
    mods = jnp.transpose(mod_table, (1, 0, 2))
    spread_shapes = (shape((count, width)), shape((count, half)), shape((count, half)))

    sources = (up_a.T, down_b, up_b, down_a.T, step_index, latents, mods)
    p_own, q_own, normed = call(
        functools.partial(prepare_body, dp, rank),
        (
            shape((height, extra)),
            shape((height, hidden)),
            shape((count, width)),
        ),
        [HBM] * 7,
        (VMEM,) * 3,
        "prepare",
        [(pltpu.SMEM if a is step_index else pltpu.VMEM)(a.shape, a.dtype) for a in sources]
        + [pltpu.SemaphoreType.DMA((7,))],
    )(*[pinned(a, pltpu.HBM) for a in sources])

    def fetch(start, name):
        return call(
            functools.partial(fetch_body, start),
            pltpu.VMEM((width, hidden // 2), BF16),
            [HBM],
            VMEM,
            name,
            [pltpu.SemaphoreType.DMA((STREAMS,))],
            bytes_accessed=base_up.size * 2,
        )(pinned(base_up, pltpu.HBM))

    p_line = jnp.concatenate([p_own] + [swap(p_own, "tp", k) for k in (1, 2, 3)], axis=1)
    up_0, up_1 = fetch(0, "fetch_up_0"), fetch(hidden // 2, "fetch_up_1")
    p_line, up_0, up_1 = lax.optimization_barrier((p_line, up_0, up_1))
    p_far = swap(p_line, "dp", 2)
    q_far = swap(q_own, "dp", 2)
    tokens = [normed] + [swap(normed, "tp", k) for k in TOKEN_ORDER]
    p_far, q_far, tokens = lax.optimization_barrier((p_far, q_far, tokens))
    near = [swap(a, "dp", 1) for a in (p_line, q_own, p_far, q_far)]
    factors = call(
        functools.partial(assemble_body, tp, dp),
        (
            pltpu.VMEM((width, both), BF16),
            pltpu.VMEM((both, hidden), BF16),
            pltpu.VMEM((both, width), BF16),
            pltpu.VMEM((hidden, both), BF16),
        ),
        [VMEM] * (2 * dp),
        (VMEM,) * 4,
        "assemble_factors",
    )(p_line, near[0], p_far, near[2], q_own, near[1], q_far, near[3])
    resident = [pinned(a, pltpu.VMEM) for a in (*factors, up_0, up_1)]

    def block(parts, downs):
        streamed = downs is None
        given = [pinned(base_down, pltpu.HBM)] if streamed else [pinned(a, pltpu.VMEM) for a in downs]
        return call(
            functools.partial(block_body, streamed, rank),
            (
                shape((count, width), F32),
                shape((count, width)),
                shape((count, half)),
                shape((count, half), F32),
                shape((count, half)),
                shape((count, half)),
            )
            + (pltpu.VMEM((hidden, half), BF16),) * (2 * streamed),
            [VMEM] * (len(parts) + 6) + [HBM if streamed else VMEM] * len(given),
            (VMEM,) * (6 + 2 * streamed),
            "block",
            [pltpu.VMEM((rows, width), BF16), pltpu.VMEM((rows, hidden), BF16)]
            + [pltpu.SemaphoreType.DMA((2, STREAMS))] * streamed,
            flops=4 * rows * width * hidden,
            bytes_accessed=4 * width * hidden,
        )(*parts, *resident, *given)

    tokens = [tokens[0]] + [tokens[1 + TOKEN_ORDER.index(k)] for k in (1, 2, 3)]
    *sums, down_0, down_1 = block(tokens, None)
    vel, state, normed, far, rest = call(
        middle_body,
        (shape((count, width), F32), shape((count, width), F32)) + spread_shapes,
        [SMEM] + [VMEM] * 7,
        (VMEM,) * 5,
        "first_update",
    )(step_index, latents, mods, *reduce(*sums))
    far = swap(far, "tp", 2)
    sums = block(gather(normed, spread(normed, rest, far), far), (down_0, down_1))
    return call(
        last_body,
        (shape((2, count, width), F32), shape((count, width), F32)),
        [SMEM] + [VMEM] * 8,
        (VMEM,) * 2,
        "second_update",
    )(step_index, mods, vel, state, *reduce(*sums))


def normalize(state, shift, scale):
    mean = jnp.mean(state, axis=1, keepdims=True)
    centered = state - mean
    spread = jnp.mean(centered * centered, axis=1, keepdims=True)
    return (centered * lax.rsqrt(spread + 1e-06) * (1.0 + scale) + shift).astype(jnp.bfloat16)


def plain(latents, step_index, mod_table, base_up, base_down, up_a, up_b, down_a, down_b):
    full_up_a, full_down_b = (
        lax.all_gather(up_a, ("dp", "tp"), axis=0, tiled=True),
        lax.all_gather(down_b, ("dp", "tp"), axis=1, tiled=True),
    )
    cols_up_b, rows_down_a = (
        lax.all_gather(up_b, "dp", axis=0, tiled=True),
        lax.all_gather(down_a, "dp", axis=1, tiled=True),
    )
    merged_up = (
        base_up.astype(jnp.float32)
        + jnp.dot(full_up_a, cols_up_b, preferred_element_type=jnp.float32)
    ).astype(jnp.bfloat16)
    merged_down = (
        base_down.astype(jnp.float32)
        + jnp.dot(rows_down_a, full_down_b, preferred_element_type=jnp.float32)
    ).astype(jnp.bfloat16)
    own_count = latents.shape[0]
    group_rows = own_count * lax.axis_size("tp")
    image_count = step_index.shape[0]
    image_rows = group_rows // image_count
    own_start = lax.axis_index("tp") * own_count
    step_size = -1.0 / NSTEPS

    def row_steps(count, offset):
        rows = jnp.arange(count, dtype=jnp.int32)
        image = rows // image_rows
        picks = (image[:, None] == jnp.arange(image_count, dtype=jnp.int32)[None, :]).astype(
            jnp.int32
        )
        return jnp.sum(picks * step_index[None, :], axis=1) + offset

    def modulation(steps):
        onehot = (steps[:, None] == jnp.arange(NSTEPS, dtype=jnp.int32)[None, :]).astype(
            jnp.float32
        )
        shift = jnp.dot(onehot, mod_table[:, 0, :], precision=lax.Precision.HIGHEST)
        scale = jnp.dot(onehot, mod_table[:, 1, :], precision=lax.Precision.HIGHEST)
        gate = jnp.dot(onehot, mod_table[:, 2, :], precision=lax.Precision.HIGHEST)
        return (shift, scale, gate)

    def project(normed):
        upper = jnp.dot(normed, merged_up, preferred_element_type=jnp.float32)
        hidden = jax.nn.gelu(upper, approximate=True).astype(jnp.bfloat16)
        return jnp.dot(hidden, merged_down, preferred_element_type=jnp.float32)

    state_all = lax.all_gather(latents, "tp", axis=0, tiled=True).astype(jnp.float32)
    shift, scale, gate = modulation(row_steps(group_rows, 0))
    normed = normalize(state_all, shift, scale)
    first = gate * lax.psum(project(normed), "tp")
    state_all = state_all + step_size * first
    shift, scale, gate = modulation(row_steps(group_rows, 1))
    normed = normalize(state_all, shift, scale)
    gate_own = lax.dynamic_slice_in_dim(gate, own_start, own_count, 0)
    second = gate_own * lax.psum_scatter(project(normed), "tp", scatter_dimension=0, tiled=True)
    state_own = lax.dynamic_slice_in_dim(state_all, own_start, own_count, 0) + step_size * second
    first_own = lax.dynamic_slice_in_dim(first, own_start, own_count, 0)
    return (jnp.stack([first_own, second]), state_own)


def solution(mesh):
    tp, dp = mesh.shape["tp"], mesh.shape["dp"]

    def local(*args):
        latents, step_index, mod_table, base_up, base_down, up_a, up_b = args[:7]
        whole_tiles = (
            tp == 4
            and dp == 4
            and latents.shape[0] == 2 * up_b.shape[0]
            and base_up.shape[1] % 256 == 0
            and base_up.shape[0] % 256 == 0
            and up_b.shape[0] % 16 == 0
            and up_a.shape[0] % (2 * up_b.shape[0]) == 0
            and tp % step_index.shape[0] == 0
        )
        return (fast if whole_tiles else plain)(*args)

    return jax.shard_map(
        local,
        mesh=mesh,
        in_specs=(
            P(("grp", "dp", "tp"), None),
            P(("grp", "dp")),
            P(),
            P(None, "tp"),
            P("tp", None),
            P(("dp", "tp"), None),
            P("dp", "tp"),
            P("tp", "dp"),
            P(None, ("dp", "tp")),
        ),
        out_specs=(P(None, ("grp", "dp", "tp"), None), P(("grp", "dp", "tp"), None)),
        check_vma=False,
    )
```

```python
import functools

import jax
import jax.numpy as jnp
from jax import lax
from jax.experimental import pallas as pl
from jax.experimental.pallas import tpu as pltpu
from jax.sharding import PartitionSpec as P

NSTEPS = 4
STREAMS = 4
STEP_SIZE = -1.0 / NSTEPS
BF16, F32 = jnp.bfloat16, jnp.float32
VMEM_GRANT = 4 << 20
VMEM = pl.BlockSpec(memory_space=pltpu.VMEM)
SMEM = pl.BlockSpec(memory_space=pltpu.SMEM)
HBM = pl.BlockSpec(memory_space=pltpu.HBM)
NT = (((1,), (1,)), ((), ()))


def call(body, outs, in_specs, out_specs, name, scratch=(), flops=0, bytes_accessed=0):
    return pl.pallas_call(
        body,
        out_shape=outs,
        in_specs=in_specs,
        out_specs=out_specs,
        scratch_shapes=list(scratch),
        compiler_params=pltpu.CompilerParams(vmem_limit_bytes=VMEM_GRANT),
        cost_estimate=pl.CostEstimate(
            flops=flops, bytes_accessed=bytes_accessed, transcendentals=0
        ),
        name=name,
    )


def shape(dims, dtype=BF16):
    return jax.ShapeDtypeStruct(dims, dtype)


def modulated(state, shift, scale):
    mean = jnp.mean(state, axis=1, keepdims=True)
    centered = state - mean
    spread = jnp.mean(centered * centered, axis=1, keepdims=True)
    return (centered * lax.rsqrt(spread + 1e-06) * (1.0 + scale) + shift).astype(BF16)


def spread_out(normed, out_ref, far_ref, rest_ref):
    half = far_ref.shape[1]
    out_ref[...] = normed
    far_ref[...] = normed[:, :half]
    rest_ref[...] = normed[:, half:]


def gelu(x):
    return x * (0.5 * (1.0 + jnp.tanh(0.7978845608028654 * (x + 0.044715 * (x * x * x)))))


def own_image(count, images):
    tp = lax.axis_size("tp")
    return lax.axis_index("tp") * images // tp


def mod_row(mod_ref, which, step):
    return mod_ref[which, pl.ds(step, 1), :]


def prepare_body(slots, rank, *refs):
    sources, outs, held, sems = refs[:7], refs[7:12], refs[12:19], refs[-1]
    copies = [
        pltpu.make_async_copy(src, dst, sems.at[i])
        for i, (src, dst) in enumerate(zip(sources, held))
    ]
    for copy in copies:
        copy.start()
    for copy in copies:
        copy.wait()
    ua_ref, db_ref, ub_ref, da_ref, steps_ref, lat_ref, mod_ref = held
    p_ref, q_ref = outs[:2]
    rows = []
    for slot in range(slots):
        part = pl.ds(slot * rank, rank)
        rows += [ua_ref[part, :], db_ref[part, :]]
    both = jnp.concatenate(rows, axis=0)
    width = both.shape[0]
    eye = (
        lax.broadcasted_iota(jnp.int32, (width, width), 0)
        == lax.broadcasted_iota(jnp.int32, (width, width), 1)
    ).astype(F32)
    cols = lax.dot_general(
        both, eye.astype(BF16), (((0,), (0,)), ((), ())), preferred_element_type=F32
    ).astype(BF16)
    height = p_ref.shape[0]
    for piece in range(cols.shape[0] // height):
        p_ref[:, piece * width : (piece + 1) * width] = cols[piece * height : (piece + 1) * height, :]
    q_ref[0:rank, :] = ub_ref[...]
    q_ref[rank : 2 * rank, :] = da_ref[...]
    step = steps_ref[own_image(lat_ref.shape[0], steps_ref.shape[0])]
    state = lat_ref[...].astype(F32)
    spread_out(modulated(state, mod_row(mod_ref, 0, step), mod_row(mod_ref, 1, step)), *outs[2:])


def fetch_body(start, source, target, sems):
    copies = stream_copies(source, target, sems, start)
    for copy in copies:
        copy.start()
    for copy in copies:
        copy.wait()


def assemble_body(tp, dp, *refs):
    p_parts, q_parts, (p_ref, q_ref, pt_ref, qt_ref) = refs[:dp], refs[dp : 2 * dp], refs[2 * dp :]
    me_tp, me_dp = lax.axis_index("tp"), lax.axis_index("dp")
    height = q_parts[0].shape[0]
    width = p_ref.shape[1]
    per_block = p_ref.shape[0] // (tp * dp)
    pieces = per_block // height
    for j in range(dp):
        owner = me_dp ^ j
        q_ref[pl.ds(pl.multiple_of(owner * height, height), height), :] = q_parts[j][...]
        for k in range(tp):
            base = (owner * tp + (me_tp ^ k)) * per_block
            for piece in range(pieces):
                col = (k * pieces + piece) * width
                p_ref[pl.ds(pl.multiple_of(base + piece * height, height), height), :] = p_parts[j][
                    :, col : col + width
                ]
    pt_ref[...] = p_ref[...].T
    qt_ref[...] = q_ref[...].T


def stream_copies(source, target, sems, start):
    rows = target.shape[0] // STREAMS
    copies = []
    for i in range(STREAMS):
        block = pl.ds(i * rows, rows)
        copies.append(
            pltpu.make_async_copy(
                source.at[block, pl.ds(start, target.shape[1])], target.at[block], sems.at[i]
            )
        )
    return copies


def start_stream(source, target, sems, start):
    rows = target.shape[0] // STREAMS
    cols = pl.ds(start, target.shape[1])

    @pl.loop(0, STREAMS)
    def _(i):
        block = pl.ds(pl.multiple_of(i * rows, rows), rows)
        pltpu.make_async_copy(source.at[block, cols], target.at[block], sems.at[i]).start()


def block_body(rank, *refs):
    x_refs, (p_ref, q_ref, pt_ref, qt_ref, wu_ref, wd_ref), refs = refs[:6], refs[6:12], refs[12:]
    outs, (x_all, hidden) = refs[:6], refs[6:]
    count, width = x_refs[0].shape
    half = width // 2
    own_ref, near_ref, far_ref, over_ref, rest_2_ref, rest_3_ref = x_refs
    x_all[:count, :] = own_ref[...]
    x_all[count : 2 * count, :] = near_ref[...]
    x_all[2 * count : 3 * count, :half] = far_ref[...]
    x_all[2 * count : 3 * count, half:] = rest_2_ref[...]
    x_all[3 * count :, :half] = over_ref[...]
    x_all[3 * count :, half:] = rest_3_ref[...]
    lanes = lax.broadcasted_iota(jnp.int32, (1, p_ref.shape[1]), 1)
    first_half = (lanes // rank) % 2 == 0
    low = jnp.dot(x_all[...], p_ref[...], preferred_element_type=F32)
    low = jnp.where(first_half, low, 0.0).astype(BF16)
    tile = hidden.shape[1] // 2
    for i in range(2):
        cols = slice(i * tile, (i + 1) * tile)
        upper = jnp.dot(x_all[...], wu_ref[:, cols], preferred_element_type=F32)
        upper += jnp.dot(low, q_ref[:, cols], preferred_element_type=F32)
        hidden[:, cols] = gelu(upper).astype(BF16)
    low = jnp.dot(hidden[...], qt_ref[...], preferred_element_type=F32)
    low = jnp.where(first_half, 0.0, low).astype(BF16)
    own_out, near_out, over_out, far_out, rest_2_out, rest_3_out = outs
    for i in range(2):
        cols = slice(i * half, (i + 1) * half)
        out = jnp.dot(hidden[...], wd_ref[:, cols], preferred_element_type=F32)
        out += jnp.dot(low, pt_ref[:, cols], preferred_element_type=F32)
        own_out[:, cols] = out[:count]
        near_out[:, cols] = out[count : 2 * count].astype(BF16)
        if i == 0:
            far_out[...] = out[2 * count : 3 * count]
            over_out[...] = out[3 * count :].astype(BF16)
        else:
            rest_2_out[...] = out[2 * count : 3 * count].astype(BF16)
            rest_3_out[...] = out[3 * count :].astype(BF16)


def relay_body(mine_ref, got_ref, out_ref):
    out_ref[...] = (mine_ref[...] + got_ref[...].astype(F32)).astype(BF16)


def summed(own_ref, near_ref, far_ref, rest_2_ref, rest_3_ref):
    half = far_ref.shape[1]
    total = own_ref[...] + near_ref[...].astype(F32)
    first = total[:, :half] + far_ref[...].astype(F32)
    second = total[:, half:] + rest_2_ref[...].astype(F32) + rest_3_ref[...].astype(F32)
    return jnp.concatenate([first, second], axis=1)


def middle_body(steps_ref, lat_ref, mod_ref, *refs):
    parts, (vel_ref, state_ref, out_ref, far_ref, rest_ref) = refs[:5], refs[5:]
    step = steps_ref[own_image(lat_ref.shape[0], steps_ref.shape[0])]
    vel = mod_row(mod_ref, 2, step) * summed(*parts)
    state = lat_ref[...].astype(F32) + STEP_SIZE * vel
    vel_ref[...] = vel
    state_ref[...] = state
    normed = modulated(state, mod_row(mod_ref, 0, step + 1), mod_row(mod_ref, 1, step + 1))
    spread_out(normed, out_ref, far_ref, rest_ref)


def last_body(steps_ref, mod_ref, vel_ref, state_ref, *refs):
    parts, (vels_ref, out_ref) = refs[:-2], refs[-2:]
    step = steps_ref[own_image(out_ref.shape[0], steps_ref.shape[0])] + 1
    vel = mod_row(mod_ref, 2, step) * summed(*parts)
    vels_ref[0] = vel_ref[...]
    vels_ref[1] = vel
    out_ref[...] = state_ref[...] + STEP_SIZE * vel


def swap(x, axis, flip):
    return lax.ppermute(x, axis, [(i, i ^ flip) for i in range(lax.axis_size(axis))])


def spread(whole, rest, far):
    return dict(
        over=swap(far, "tp", 1),
        near=swap(whole, "tp", 1),
        rest_2=swap(rest, "tp", 2),
        rest_3=swap(rest, "tp", 3),
    )


def gather(own, got, far):
    return [own, got["near"], far, got["over"], got["rest_2"], got["rest_3"]]


def reduce(own, near, over, far, rest_2, rest_3):
    rest_2 = swap(rest_2, "tp", 2)
    rest_3 = swap(rest_3, "tp", 3)
    over = swap(over, "tp", 1)
    over, rest_2 = lax.optimization_barrier((over, rest_2))
    relayed = call(relay_body, shape(far.shape), [VMEM] * 2, VMEM, "relay")(far, over)
    relayed = swap(relayed, "tp", 2)
    near = swap(near, "tp", 1)
    return own, near, relayed, rest_2, rest_3


def pinned(x, space):
    return pltpu.with_memory_space_constraint(x, space)


def fast(latents, step_index, mod_table, base_up, base_down, up_a, up_b, down_a, down_b):
    tp, dp = lax.axis_size("tp"), lax.axis_size("dp")
    count, width = latents.shape
    rows = count * tp
    half = width // 2
    hidden = base_up.shape[1]
    rank = up_b.shape[0]
    both = 2 * rank * dp
    height = 2 * rank
    extra = up_a.shape[0] // height * both
    mods = jnp.transpose(mod_table, (1, 0, 2))
    spread_shapes = (shape((count, width)), shape((count, half)), shape((count, half)))

    sources = (up_a.T, down_b, up_b, down_a.T, step_index, latents, mods)
    p_own, q_own, normed, far, rest = call(
        functools.partial(prepare_body, dp, rank),
        (
            shape((height, extra)),
            shape((height, hidden)),
        )
        + spread_shapes,
        [HBM] * 7,
        (VMEM,) * 5,
        "prepare",
        flops=16 * rows * width * hidden,

        scratch=[(pltpu.SMEM if a is step_index else pltpu.VMEM)(a.shape, a.dtype) for a in sources]
        + [pltpu.SemaphoreType.DMA((7,))],
    )(*[pinned(a, pltpu.HBM) for a in sources])

    def fetch(start, name):
        return call(
            functools.partial(fetch_body, start),
            pltpu.VMEM((width, hidden // 2), BF16),
            [HBM],
            VMEM,
            name,
            [pltpu.SemaphoreType.DMA((STREAMS,))],
            bytes_accessed=base_up.size * 2,
        )(pinned(base_up, pltpu.HBM))

    far = swap(far, "tp", 2)
    p_line = jnp.concatenate([p_own] + [swap(p_own, "tp", k) for k in (1, 2, 3)], axis=1)
    p_line, q_own = lax.optimization_barrier((p_line, q_own))
    p_far = swap(p_line, "dp", 2)
    q_far = swap(q_own, "dp", 2)
    got = spread(normed, rest, far)
    keys = ("near", "rest_2", "rest_3", "over")
    p_far, q_far, held = lax.optimization_barrier((p_far, q_far, [got[k] for k in keys]))
    got.update(zip(keys, held))
    near = [swap(a, "dp", 1) for a in (p_line, q_own, p_far, q_far)]
    factors = call(
        functools.partial(assemble_body, tp, dp),
        (
            pltpu.VMEM((width, both), BF16),
            pltpu.VMEM((both, hidden), BF16),
            pltpu.VMEM((both, width), BF16),
            pltpu.VMEM((hidden, both), BF16),
        ),
        [VMEM] * (2 * dp),
        (VMEM,) * 4,
        "assemble_factors",
    )(p_line, near[0], p_far, near[2], q_own, near[1], q_far, near[3])
    resident = [pinned(a, pltpu.VMEM) for a in (*factors, base_up, base_down)]

    def block(parts):
        return call(
            functools.partial(block_body, rank),
            (
                shape((count, width), F32),
                shape((count, width)),
                shape((count, half)),
                shape((count, half), F32),
                shape((count, half)),
                shape((count, half)),
            ),
            [VMEM] * 12,
            (VMEM,) * 6,
            "block",
            [pltpu.VMEM((rows, width), BF16), pltpu.VMEM((rows, hidden), BF16)],
            flops=4 * rows * width * hidden,
            bytes_accessed=4 * width * hidden,
        )(*parts, *resident)

    sums = block(gather(normed, got, far))
    vel, state, normed, far, rest = call(
        middle_body,
        (shape((count, width), F32), shape((count, width), F32)) + spread_shapes,
        [SMEM] + [VMEM] * 7,
        (VMEM,) * 5,
        "first_update",
    )(step_index, latents, mods, *reduce(*sums))
    far = swap(far, "tp", 2)
    sums = block(gather(normed, spread(normed, rest, far), far))
    return call(
        last_body,
        (shape((2, count, width), F32), shape((count, width), F32)),
        [SMEM] + [VMEM] * 8,
        (VMEM,) * 2,
        "second_update",
    )(step_index, mods, vel, state, *reduce(*sums))


def normalize(state, shift, scale):
    mean = jnp.mean(state, axis=1, keepdims=True)
    centered = state - mean
    spread = jnp.mean(centered * centered, axis=1, keepdims=True)
    return (centered * lax.rsqrt(spread + 1e-06) * (1.0 + scale) + shift).astype(jnp.bfloat16)


def plain(latents, step_index, mod_table, base_up, base_down, up_a, up_b, down_a, down_b):
    full_up_a, full_down_b = (
        lax.all_gather(up_a, ("dp", "tp"), axis=0, tiled=True),
        lax.all_gather(down_b, ("dp", "tp"), axis=1, tiled=True),
    )
    cols_up_b, rows_down_a = (
        lax.all_gather(up_b, "dp", axis=0, tiled=True),
        lax.all_gather(down_a, "dp", axis=1, tiled=True),
    )
    merged_up = (
        base_up.astype(jnp.float32)
        + jnp.dot(full_up_a, cols_up_b, preferred_element_type=jnp.float32)
    ).astype(jnp.bfloat16)
    merged_down = (
        base_down.astype(jnp.float32)
        + jnp.dot(rows_down_a, full_down_b, preferred_element_type=jnp.float32)
    ).astype(jnp.bfloat16)
    own_count = latents.shape[0]
    group_rows = own_count * lax.axis_size("tp")
    image_count = step_index.shape[0]
    image_rows = group_rows // image_count
    own_start = lax.axis_index("tp") * own_count
    step_size = -1.0 / NSTEPS

    def row_steps(count, offset):
        rows = jnp.arange(count, dtype=jnp.int32)
        image = rows // image_rows
        picks = (image[:, None] == jnp.arange(image_count, dtype=jnp.int32)[None, :]).astype(
            jnp.int32
        )
        return jnp.sum(picks * step_index[None, :], axis=1) + offset

    def modulation(steps):
        onehot = (steps[:, None] == jnp.arange(NSTEPS, dtype=jnp.int32)[None, :]).astype(
            jnp.float32
        )
        shift = jnp.dot(onehot, mod_table[:, 0, :], precision=lax.Precision.HIGHEST)
        scale = jnp.dot(onehot, mod_table[:, 1, :], precision=lax.Precision.HIGHEST)
        gate = jnp.dot(onehot, mod_table[:, 2, :], precision=lax.Precision.HIGHEST)
        return (shift, scale, gate)

    def project(normed):
        upper = jnp.dot(normed, merged_up, preferred_element_type=jnp.float32)
        hidden = jax.nn.gelu(upper, approximate=True).astype(jnp.bfloat16)
        return jnp.dot(hidden, merged_down, preferred_element_type=jnp.float32)

    state_all = lax.all_gather(latents, "tp", axis=0, tiled=True).astype(jnp.float32)
    shift, scale, gate = modulation(row_steps(group_rows, 0))
    normed = normalize(state_all, shift, scale)
    first = gate * lax.psum(project(normed), "tp")
    state_all = state_all + step_size * first
    shift, scale, gate = modulation(row_steps(group_rows, 1))
    normed = normalize(state_all, shift, scale)
    gate_own = lax.dynamic_slice_in_dim(gate, own_start, own_count, 0)
    second = gate_own * lax.psum_scatter(project(normed), "tp", scatter_dimension=0, tiled=True)
    state_own = lax.dynamic_slice_in_dim(state_all, own_start, own_count, 0) + step_size * second
    first_own = lax.dynamic_slice_in_dim(first, own_start, own_count, 0)
    return (jnp.stack([first_own, second]), state_own)


def solution(mesh):
    tp, dp = mesh.shape["tp"], mesh.shape["dp"]

    def local(*args):
        latents, step_index, mod_table, base_up, base_down, up_a, up_b = args[:7]
        whole_tiles = (
            tp == 4
            and dp == 4
            and latents.shape[0] == 2 * up_b.shape[0]
            and base_up.shape[1] % 256 == 0
            and base_up.shape[0] % 256 == 0
            and up_b.shape[0] % 16 == 0
            and up_a.shape[0] % (2 * up_b.shape[0]) == 0
            and tp % step_index.shape[0] == 0
        )
        return (fast if whole_tiles else plain)(*args)

    return jax.shard_map(
        local,
        mesh=mesh,
        in_specs=(
            P(("grp", "dp", "tp"), None),
            P(("grp", "dp")),
            P(),
            P(None, "tp"),
            P("tp", None),
            P(("dp", "tp"), None),
            P("dp", "tp"),
            P("tp", "dp"),
            P(None, ("dp", "tp")),
        ),
        out_specs=(P(None, ("grp", "dp", "tp"), None), P(("grp", "dp", "tp"), None)),
        check_vma=False,
    )
```

```python
import functools

import jax
import jax.numpy as jnp
from jax import lax
from jax.experimental import pallas as pl
from jax.experimental.pallas import tpu as pltpu
from jax.sharding import PartitionSpec as P

NSTEPS = 4
STEP_SIZE = -1.0 / NSTEPS
BF16, F32 = jnp.bfloat16, jnp.float32
VMEM_GRANT = 4 << 20
VMEM = pl.BlockSpec(memory_space=pltpu.VMEM)
SMEM = pl.BlockSpec(memory_space=pltpu.SMEM)
HBM = pl.BlockSpec(memory_space=pltpu.HBM)
NT = (((1,), (1,)), ((), ()))


def call(body, outs, in_specs, out_specs, name, scratch=(), flops=0, bytes_accessed=0):
    return pl.pallas_call(
        body,
        out_shape=outs,
        in_specs=in_specs,
        out_specs=out_specs,
        scratch_shapes=list(scratch),
        compiler_params=pltpu.CompilerParams(vmem_limit_bytes=VMEM_GRANT),
        cost_estimate=pl.CostEstimate(
            flops=flops, bytes_accessed=bytes_accessed, transcendentals=0
        ),
        name=name,
    )


def shape(dims, dtype=BF16):
    return jax.ShapeDtypeStruct(dims, dtype)


def modulated(state, shift, scale):
    mean = jnp.mean(state, axis=1, keepdims=True)
    centered = state - mean
    spread = jnp.mean(centered * centered, axis=1, keepdims=True)
    return (centered * lax.rsqrt(spread + 1e-06) * (1.0 + scale) + shift).astype(BF16)


def spread_out(normed, out_ref, far_ref, rest_ref):
    half = far_ref.shape[1]
    out_ref[...] = normed
    far_ref[...] = normed[:, :half]
    rest_ref[...] = normed[:, half:]


def gelu(x):
    return x * (0.5 * (1.0 + jnp.tanh(0.7978845608028654 * (x + 0.044715 * (x * x * x)))))


def own_image(images):
    tp = lax.axis_size("tp")
    return lax.axis_index("tp") * images // tp


def mod_row(mod_ref, which, step):
    return mod_ref[which, pl.ds(step, 1), :]


def prepare_body(slots, rank, *refs):
    sources, outs, held, sems = refs[:7], refs[7:12], refs[12:19], refs[-1]
    copies = [
        pltpu.make_async_copy(src, dst, sems.at[i])
        for i, (src, dst) in enumerate(zip(sources, held))
    ]
    for copy in copies:
        copy.start()
    for copy in copies:
        copy.wait()
    ua_ref, db_ref, ub_ref, da_ref, steps_ref, lat_ref, mod_ref = held
    p_ref, q_ref = outs[:2]
    rows = []
    for slot in range(slots):
        part = pl.ds(slot * rank, rank)
        rows += [ua_ref[part, :], db_ref[part, :]]
    both = jnp.concatenate(rows, axis=0)
    width = both.shape[0]
    eye = (
        lax.broadcasted_iota(jnp.int32, (width, width), 0)
        == lax.broadcasted_iota(jnp.int32, (width, width), 1)
    ).astype(F32)
    cols = lax.dot_general(
        both, eye.astype(BF16), (((0,), (0,)), ((), ())), preferred_element_type=F32
    ).astype(BF16)
    height = p_ref.shape[0]
    for piece in range(cols.shape[0] // height):
        p_ref[:, piece * width : (piece + 1) * width] = cols[piece * height : (piece + 1) * height, :]
    q_ref[0:rank, :] = ub_ref[...]
    q_ref[rank : 2 * rank, :] = da_ref[...]
    step = steps_ref[own_image(steps_ref.shape[0])]
    state = lat_ref[...].astype(F32)
    spread_out(modulated(state, mod_row(mod_ref, 0, step), mod_row(mod_ref, 1, step)), *outs[2:])


def assemble_body(tp, dp, *refs):
    p_parts, q_parts, (p_ref, q_ref, pt_ref, qt_ref) = refs[:dp], refs[dp : 2 * dp], refs[2 * dp :]
    me_tp, me_dp = lax.axis_index("tp"), lax.axis_index("dp")
    height = q_parts[0].shape[0]
    width = p_ref.shape[1]
    per_block = p_ref.shape[0] // (tp * dp)
    pieces = per_block // height
    for j in range(dp):
        owner = me_dp ^ j
        q_ref[pl.ds(pl.multiple_of(owner * height, height), height), :] = q_parts[j][...]
        for k in range(tp):
            base = (owner * tp + (me_tp ^ k)) * per_block
            for piece in range(pieces):
                col = (k * pieces + piece) * width
                p_ref[pl.ds(pl.multiple_of(base + piece * height, height), height), :] = p_parts[j][
                    :, col : col + width
                ]
    pt_ref[...] = p_ref[...].T
    qt_ref[...] = q_ref[...].T


def block_body(rank, *refs):
    x_refs, (p_ref, q_ref, pt_ref, qt_ref, wu_ref, wd_ref), refs = refs[:6], refs[6:12], refs[12:]
    outs, (x_all, hidden) = refs[:6], refs[6:]
    count, width = x_refs[0].shape
    half = width // 2
    own_ref, near_ref, far_ref, over_ref, rest_2_ref, rest_3_ref = x_refs
    x_all[:count, :] = own_ref[...]
    x_all[count : 2 * count, :] = near_ref[...]
    x_all[2 * count : 3 * count, :half] = far_ref[...]
    x_all[2 * count : 3 * count, half:] = rest_2_ref[...]
    x_all[3 * count :, :half] = over_ref[...]
    x_all[3 * count :, half:] = rest_3_ref[...]
    lanes = lax.broadcasted_iota(jnp.int32, (1, p_ref.shape[1]), 1)
    first_half = (lanes // rank) % 2 == 0
    low = jnp.dot(x_all[...], p_ref[...], preferred_element_type=F32)
    low = jnp.where(first_half, low, 0.0).astype(BF16)
    tile = hidden.shape[1] // 3
    for i in range(3):
        cols = slice(i * tile, (i + 1) * tile)
        upper = jnp.dot(x_all[...], wu_ref[:, cols], preferred_element_type=F32)
        upper += jnp.dot(low, q_ref[:, cols], preferred_element_type=F32)
        hidden[:, cols] = gelu(upper).astype(BF16)
    low = jnp.dot(hidden[...], qt_ref[...], preferred_element_type=F32)
    low = jnp.where(first_half, 0.0, low).astype(BF16)
    own_out, near_out, over_out, far_out, rest_2_out, rest_3_out = outs
    for i in range(2):
        cols = slice(i * half, (i + 1) * half)
        out = jnp.dot(hidden[...], wd_ref[:, cols], preferred_element_type=F32)
        out += jnp.dot(low, pt_ref[:, cols], preferred_element_type=F32)
        own_out[:, cols] = out[:count]
        near_out[:, cols] = out[count : 2 * count].astype(BF16)
        if i == 0:
            far_out[...] = out[2 * count : 3 * count]
            over_out[...] = out[3 * count :].astype(BF16)
        else:
            rest_2_out[...] = out[2 * count : 3 * count].astype(BF16)
            rest_3_out[...] = out[3 * count :].astype(BF16)


def relay_body(mine_ref, got_ref, out_ref):
    out_ref[...] = (mine_ref[...] + got_ref[...].astype(F32)).astype(BF16)


def summed(own_ref, near_ref, far_ref, rest_2_ref, rest_3_ref):
    half = far_ref.shape[1]
    total = own_ref[...] + near_ref[...].astype(F32)
    first = total[:, :half] + far_ref[...].astype(F32)
    second = total[:, half:] + rest_2_ref[...].astype(F32) + rest_3_ref[...].astype(F32)
    return first, second


def middle_body(steps_ref, lat_ref, mod_ref, *refs):
    parts, (vel_ref, state_ref, out_ref, far_ref, rest_ref) = refs[:5], refs[5:]
    step = steps_ref[own_image(steps_ref.shape[0])]
    vel = mod_row(mod_ref, 2, step) * jnp.concatenate(summed(*parts), axis=1)
    state = lat_ref[...].astype(F32) + STEP_SIZE * vel
    vel_ref[...] = vel
    state_ref[...] = state
    normed = modulated(state, mod_row(mod_ref, 0, step + 1), mod_row(mod_ref, 1, step + 1))
    spread_out(normed, out_ref, far_ref, rest_ref)


def last_body(steps_ref, mod_ref, vel_ref, state_ref, *refs):
    parts, (vels_ref, out_ref, vel_held, state_held, sems) = refs[:5], refs[5:]
    copies = [pltpu.make_async_copy(vel_ref, vels_ref.at[0], sems.at[0])]
    copies[0].start()
    step = steps_ref[own_image(steps_ref.shape[0])] + 1
    gate = mod_row(mod_ref, 2, step)
    half = state_ref.shape[1] // 2
    for i, total in enumerate(summed(*parts)):
        cols = slice(i * half, (i + 1) * half)
        vel = gate[:, cols] * total
        vel_held[:, cols] = vel
        state_held[:, cols] = state_ref[:, cols] + STEP_SIZE * vel
        place = (slice(None), pl.ds(i * half, half))
        for k, (source, target) in enumerate(((vel_held, vels_ref.at[1]), (state_held, out_ref))):
            copies.append(
                pltpu.make_async_copy(source.at[place], target.at[place], sems.at[1 + 2 * i + k])
            )
            copies[-1].start()
    for copy in copies:
        copy.wait()


def swap(x, axis, flip):
    return lax.ppermute(x, axis, [(i, i ^ flip) for i in range(lax.axis_size(axis))])


def spread(whole, rest, far):
    return dict(
        over=swap(far, "tp", 1),
        near=swap(whole, "tp", 1),
        rest_2=swap(rest, "tp", 2),
        rest_3=swap(rest, "tp", 3),
    )


def gather(own, got, far):
    return [own, got["near"], far, got["over"], got["rest_2"], got["rest_3"]]


def reduce(own, near, over, far, rest_2, rest_3):
    rest_2 = swap(rest_2, "tp", 2)
    rest_3 = swap(rest_3, "tp", 3)
    over = swap(over, "tp", 1)
    over, rest_2 = lax.optimization_barrier((over, rest_2))
    relayed = call(relay_body, shape(far.shape), [VMEM] * 2, VMEM, "relay")(far, over)
    relayed = swap(relayed, "tp", 2)
    near = swap(near, "tp", 1)
    return own, near, relayed, rest_2, rest_3


def pinned(x, space):
    return pltpu.with_memory_space_constraint(x, space)


def fast(latents, step_index, mod_table, base_up, base_down, up_a, up_b, down_a, down_b):
    tp, dp = lax.axis_size("tp"), lax.axis_size("dp")
    count, width = latents.shape
    rows = count * tp
    half = width // 2
    hidden = base_up.shape[1]
    rank = up_b.shape[0]
    both = 2 * rank * dp
    height = 2 * rank
    mods = jnp.transpose(mod_table, (1, 0, 2))
    spread_shapes = (shape((count, width)), shape((count, half)), shape((count, half)))

    sources = (up_a.T, down_b, up_b, down_a.T, step_index, latents, mods)
    p_own, q_own, normed, far, rest = call(
        functools.partial(prepare_body, dp, rank),
        (
            shape((height, up_a.shape[0] // height * both)),
            shape((height, hidden)),
        )
        + spread_shapes,
        [HBM] * 7,
        (VMEM,) * 5,
        "prepare",
        flops=16 * rows * width * hidden,
        scratch=[(pltpu.SMEM if a is step_index else pltpu.VMEM)(a.shape, a.dtype) for a in sources]
        + [pltpu.SemaphoreType.DMA((7,))],
    )(*[pinned(a, pltpu.HBM) for a in sources])

    far = swap(far, "tp", 2)
    p_line = jnp.concatenate([p_own] + [swap(p_own, "tp", k) for k in (1, 2, 3)], axis=1)
    p_line, q_own = lax.optimization_barrier((p_line, q_own))
    p_far = swap(p_line, "dp", 2)
    q_far = swap(q_own, "dp", 2)
    got = spread(normed, rest, far)
    keys = ("near", "rest_2", "rest_3", "over")
    p_far, q_far, held = lax.optimization_barrier((p_far, q_far, [got[k] for k in keys]))
    got.update(zip(keys, held))
    near = [swap(a, "dp", 1) for a in (p_line, q_own, p_far, q_far)]
    factors = call(
        functools.partial(assemble_body, tp, dp),
        (
            pltpu.VMEM((width, both), BF16),
            pltpu.VMEM((both, hidden), BF16),
            pltpu.VMEM((both, width), BF16),
            pltpu.VMEM((hidden, both), BF16),
        ),
        [VMEM] * (2 * dp),
        (VMEM,) * 4,
        "assemble_factors",
    )(p_line, near[0], p_far, near[2], q_own, near[1], q_far, near[3])
    resident = [pinned(a, pltpu.VMEM) for a in (*factors, base_up, base_down)]

    def block(parts):
        return call(
            functools.partial(block_body, rank),
            (
                shape((count, width), F32),
                shape((count, width)),
                shape((count, half)),
                shape((count, half), F32),
                shape((count, half)),
                shape((count, half)),
            ),
            [VMEM] * 12,
            (VMEM,) * 6,
            "block",
            [pltpu.VMEM((rows, width), BF16), pltpu.VMEM((rows, hidden), BF16)],
            flops=4 * rows * width * hidden,
            bytes_accessed=4 * width * hidden,
        )(*parts, *resident)

    sums = block(gather(normed, got, far))
    vel, state, normed, far, rest = call(
        middle_body,
        (shape((count, width), F32), shape((count, width), F32)) + spread_shapes,
        [SMEM] + [VMEM] * 7,
        (VMEM,) * 5,
        "first_update",
    )(step_index, latents, mods, *reduce(*sums))
    far = swap(far, "tp", 2)
    sums = block(gather(normed, spread(normed, rest, far), far))
    return call(
        last_body,
        (shape((2, count, width), F32), shape((count, width), F32)),
        [SMEM] + [VMEM] * 8,
        (HBM,) * 2,
        "second_update",
        [pltpu.VMEM((count, width), F32)] * 2 + [pltpu.SemaphoreType.DMA((5,))],
    )(step_index, mods, vel, state, *reduce(*sums))


def normalize(state, shift, scale):
    mean = jnp.mean(state, axis=1, keepdims=True)
    centered = state - mean
    spread = jnp.mean(centered * centered, axis=1, keepdims=True)
    return (centered * lax.rsqrt(spread + 1e-06) * (1.0 + scale) + shift).astype(jnp.bfloat16)


def plain(latents, step_index, mod_table, base_up, base_down, up_a, up_b, down_a, down_b):
    full_up_a, full_down_b = (
        lax.all_gather(up_a, ("dp", "tp"), axis=0, tiled=True),
        lax.all_gather(down_b, ("dp", "tp"), axis=1, tiled=True),
    )
    cols_up_b, rows_down_a = (
        lax.all_gather(up_b, "dp", axis=0, tiled=True),
        lax.all_gather(down_a, "dp", axis=1, tiled=True),
    )
    merged_up = (
        base_up.astype(jnp.float32)
        + jnp.dot(full_up_a, cols_up_b, preferred_element_type=jnp.float32)
    ).astype(jnp.bfloat16)
    merged_down = (
        base_down.astype(jnp.float32)
        + jnp.dot(rows_down_a, full_down_b, preferred_element_type=jnp.float32)
    ).astype(jnp.bfloat16)
    own_count = latents.shape[0]
    group_rows = own_count * lax.axis_size("tp")
    image_count = step_index.shape[0]
    image_rows = group_rows // image_count
    own_start = lax.axis_index("tp") * own_count
    step_size = -1.0 / NSTEPS

    def row_steps(count, offset):
        rows = jnp.arange(count, dtype=jnp.int32)
        image = rows // image_rows
        picks = (image[:, None] == jnp.arange(image_count, dtype=jnp.int32)[None, :]).astype(
            jnp.int32
        )
        return jnp.sum(picks * step_index[None, :], axis=1) + offset

    def modulation(steps):
        onehot = (steps[:, None] == jnp.arange(NSTEPS, dtype=jnp.int32)[None, :]).astype(
            jnp.float32
        )
        shift = jnp.dot(onehot, mod_table[:, 0, :], precision=lax.Precision.HIGHEST)
        scale = jnp.dot(onehot, mod_table[:, 1, :], precision=lax.Precision.HIGHEST)
        gate = jnp.dot(onehot, mod_table[:, 2, :], precision=lax.Precision.HIGHEST)
        return (shift, scale, gate)

    def project(normed):
        upper = jnp.dot(normed, merged_up, preferred_element_type=jnp.float32)
        hidden = jax.nn.gelu(upper, approximate=True).astype(jnp.bfloat16)
        return jnp.dot(hidden, merged_down, preferred_element_type=jnp.float32)

    state_all = lax.all_gather(latents, "tp", axis=0, tiled=True).astype(jnp.float32)
    shift, scale, gate = modulation(row_steps(group_rows, 0))
    normed = normalize(state_all, shift, scale)
    first = gate * lax.psum(project(normed), "tp")
    state_all = state_all + step_size * first
    shift, scale, gate = modulation(row_steps(group_rows, 1))
    normed = normalize(state_all, shift, scale)
    gate_own = lax.dynamic_slice_in_dim(gate, own_start, own_count, 0)
    second = gate_own * lax.psum_scatter(project(normed), "tp", scatter_dimension=0, tiled=True)
    state_own = lax.dynamic_slice_in_dim(state_all, own_start, own_count, 0) + step_size * second
    first_own = lax.dynamic_slice_in_dim(first, own_start, own_count, 0)
    return (jnp.stack([first_own, second]), state_own)


def solution(mesh):
    tp, dp = mesh.shape["tp"], mesh.shape["dp"]

    def local(*args):
        latents, step_index, mod_table, base_up, base_down, up_a, up_b = args[:7]
        whole_tiles = (
            tp == 4
            and dp == 4
            and latents.shape[0] == 2 * up_b.shape[0]
            and base_up.shape[1] % 256 == 0
            and base_up.shape[0] % 256 == 0
            and up_b.shape[0] % 16 == 0
            and up_a.shape[0] % (2 * up_b.shape[0]) == 0
            and tp % step_index.shape[0] == 0
        )
        return (fast if whole_tiles else plain)(*args)

    return jax.shard_map(
        local,
        mesh=mesh,
        in_specs=(
            P(("grp", "dp", "tp"), None),
            P(("grp", "dp")),
            P(),
            P(None, "tp"),
            P("tp", None),
            P(("dp", "tp"), None),
            P("dp", "tp"),
            P("tp", "dp"),
            P(None, ("dp", "tp")),
        ),
        out_specs=(P(None, ("grp", "dp", "tp"), None), P(("grp", "dp", "tp"), None)),
        check_vma=False,
    )
```

```python
import functools

import jax
import jax.numpy as jnp
from jax import lax
from jax.experimental import pallas as pl
from jax.experimental.pallas import tpu as pltpu
from jax.sharding import PartitionSpec as P

NSTEPS = 4
STEP_SIZE = -1.0 / NSTEPS
BF16, F32 = jnp.bfloat16, jnp.float32
VMEM_GRANT = 4 << 20
VMEM = pl.BlockSpec(memory_space=pltpu.VMEM)
SMEM = pl.BlockSpec(memory_space=pltpu.SMEM)
HBM = pl.BlockSpec(memory_space=pltpu.HBM)
NT = (((1,), (1,)), ((), ()))


def call(body, outs, in_specs, out_specs, name, scratch=(), flops=0, bytes_accessed=0):
    return pl.pallas_call(
        body,
        out_shape=outs,
        in_specs=in_specs,
        out_specs=out_specs,
        scratch_shapes=list(scratch),
        compiler_params=pltpu.CompilerParams(vmem_limit_bytes=VMEM_GRANT),
        cost_estimate=pl.CostEstimate(
            flops=flops, bytes_accessed=bytes_accessed, transcendentals=0
        ),
        name=name,
    )


def shape(dims, dtype=BF16):
    return jax.ShapeDtypeStruct(dims, dtype)


def modulated(state, shift, scale):
    mean = jnp.mean(state, axis=1, keepdims=True)
    centered = state - mean
    spread = jnp.mean(centered * centered, axis=1, keepdims=True)
    return (centered * lax.rsqrt(spread + 1e-06) * (1.0 + scale) + shift).astype(BF16)


def spread_out(normed, out_ref, far_ref, rest_ref):
    half = far_ref.shape[1]
    out_ref[...] = normed
    far_ref[...] = normed[:, :half]
    rest_ref[...] = normed[:, half:]


def gelu(x):
    return x * (0.5 * (1.0 + jnp.tanh(0.7978845608028654 * (x + 0.044715 * (x * x * x)))))


def own_image(images):
    tp = lax.axis_size("tp")
    return lax.axis_index("tp") * images // tp


def mod_row(mod_ref, which, step):
    return mod_ref[which, pl.ds(step, 1), :]


def prepare_body(slots, rank, *refs):
    sources, outs, held, sems = refs[:7], refs[7:12], refs[12:19], refs[-1]
    copies = [
        pltpu.make_async_copy(src, dst, sems.at[i])
        for i, (src, dst) in enumerate(zip(sources, held))
    ]
    for copy in copies:
        copy.start()
    for copy in copies:
        copy.wait()
    ua_ref, db_ref, ub_ref, da_ref, steps_ref, lat_ref, mod_ref = held
    p_ref, q_ref = outs[:2]
    rows = []
    for slot in range(slots):
        part = pl.ds(slot * rank, rank)
        rows += [ua_ref[part, :], db_ref[part, :]]
    both = jnp.concatenate(rows, axis=0)
    width = both.shape[0]
    eye = (
        lax.broadcasted_iota(jnp.int32, (width, width), 0)
        == lax.broadcasted_iota(jnp.int32, (width, width), 1)
    ).astype(F32)
    cols = lax.dot_general(
        both, eye.astype(BF16), (((0,), (0,)), ((), ())), preferred_element_type=F32
    ).astype(BF16)
    height = p_ref.shape[0]
    for piece in range(cols.shape[0] // height):
        p_ref[:, piece * width : (piece + 1) * width] = cols[piece * height : (piece + 1) * height, :]
    q_ref[0:rank, :] = ub_ref[...]
    q_ref[rank : 2 * rank, :] = da_ref[...]
    step = steps_ref[own_image(steps_ref.shape[0])]
    state = lat_ref[...].astype(F32)
    spread_out(modulated(state, mod_row(mod_ref, 0, step), mod_row(mod_ref, 1, step)), *outs[2:])


def assemble_body(tp, dp, *refs):
    p_parts, q_parts, (p_ref, q_ref, pt_ref, qt_ref) = refs[:dp], refs[dp : 2 * dp], refs[2 * dp :]
    me_tp, me_dp = lax.axis_index("tp"), lax.axis_index("dp")
    height = q_parts[0].shape[0]
    width = p_ref.shape[1]
    per_block = p_ref.shape[0] // (tp * dp)
    pieces = per_block // height
    for j in range(dp):
        owner = me_dp ^ j
        q_ref[pl.ds(pl.multiple_of(owner * height, height), height), :] = q_parts[j][...]
        for k in range(tp):
            base = (owner * tp + (me_tp ^ k)) * per_block
            for piece in range(pieces):
                col = (k * pieces + piece) * width
                p_ref[pl.ds(pl.multiple_of(base + piece * height, height), height), :] = p_parts[j][
                    :, col : col + width
                ]
    pt_ref[...] = p_ref[...].T
    qt_ref[...] = q_ref[...].T


def block_body(rank, *refs):
    x_refs, (p_ref, q_ref, pt_ref, qt_ref, wu_ref, wd_ref), refs = refs[:6], refs[6:12], refs[12:]
    outs, (x_all, hidden) = refs[:6], refs[6:]
    count, width = x_refs[0].shape
    half = width // 2
    own_ref, near_ref, far_ref, over_ref, rest_2_ref, rest_3_ref = x_refs
    x_all[:count, :] = own_ref[...]
    x_all[count : 2 * count, :] = near_ref[...]
    x_all[2 * count : 3 * count, :half] = far_ref[...]
    x_all[2 * count : 3 * count, half:] = rest_2_ref[...]
    x_all[3 * count :, :half] = over_ref[...]
    x_all[3 * count :, half:] = rest_3_ref[...]
    lanes = lax.broadcasted_iota(jnp.int32, (1, p_ref.shape[1]), 1)
    first_half = (lanes // rank) % 2 == 0
    low = jnp.dot(x_all[...], p_ref[...], preferred_element_type=F32)
    low = jnp.where(first_half, low, 0.0).astype(BF16)
    tile = hidden.shape[1] // 3

    def upper(i):
        cols = slice(i * tile, (i + 1) * tile)
        out = jnp.dot(x_all[...], wu_ref[:, cols], preferred_element_type=F32)
        return out + jnp.dot(low, q_ref[:, cols], preferred_element_type=F32)

    ahead = upper(0)
    for i in range(3):
        now = ahead
        if i < 2:
            ahead = upper(i + 1)
        hidden[:, i * tile : (i + 1) * tile] = gelu(now).astype(BF16)
    low = jnp.dot(hidden[...], qt_ref[...], preferred_element_type=F32)
    low = jnp.where(first_half, 0.0, low).astype(BF16)
    own_out, near_out, over_out, far_out, rest_2_out, rest_3_out = outs
    for i in range(2):
        cols = slice(i * half, (i + 1) * half)
        out = jnp.dot(hidden[...], wd_ref[:, cols], preferred_element_type=F32)
        out += jnp.dot(low, pt_ref[:, cols], preferred_element_type=F32)
        own_out[:, cols] = out[:count]
        near_out[:, cols] = out[count : 2 * count].astype(BF16)
        if i == 0:
            far_out[...] = out[2 * count : 3 * count]
            over_out[...] = out[3 * count :].astype(BF16)
        else:
            rest_2_out[...] = out[2 * count : 3 * count].astype(BF16)
            rest_3_out[...] = out[3 * count :].astype(BF16)


def relay_body(mine_ref, got_ref, out_ref):
    out_ref[...] = (mine_ref[...] + got_ref[...].astype(F32)).astype(BF16)


def summed(own_ref, near_ref, far_ref, rest_2_ref, rest_3_ref):
    half = far_ref.shape[1]
    total = own_ref[...] + near_ref[...].astype(F32)
    first = total[:, :half] + far_ref[...].astype(F32)
    second = total[:, half:] + rest_2_ref[...].astype(F32) + rest_3_ref[...].astype(F32)
    return first, second


def middle_body(steps_ref, lat_ref, mod_ref, *refs):
    parts, (vel_ref, state_ref, out_ref, far_ref, rest_ref) = refs[:5], refs[5:]
    step = steps_ref[own_image(steps_ref.shape[0])]
    vel = mod_row(mod_ref, 2, step) * jnp.concatenate(summed(*parts), axis=1)
    state = lat_ref[...].astype(F32) + STEP_SIZE * vel
    vel_ref[...] = vel
    state_ref[...] = state
    normed = modulated(state, mod_row(mod_ref, 0, step + 1), mod_row(mod_ref, 1, step + 1))
    spread_out(normed, out_ref, far_ref, rest_ref)


def last_body(steps_ref, mod_ref, vel_ref, state_ref, *refs):
    parts, (vels_ref, out_ref, vel_held, state_held, sems) = refs[:5], refs[5:]
    copies = [pltpu.make_async_copy(vel_ref, vels_ref.at[0], sems.at[0])]
    copies[0].start()
    step = steps_ref[own_image(steps_ref.shape[0])] + 1
    gate = mod_row(mod_ref, 2, step)
    half = state_ref.shape[1] // 2
    for i, total in enumerate(summed(*parts)):
        cols = slice(i * half, (i + 1) * half)
        vel = gate[:, cols] * total
        vel_held[:, cols] = vel
        state_held[:, cols] = state_ref[:, cols] + STEP_SIZE * vel
        place = (slice(None), pl.ds(i * half, half))
        for k, (source, target) in enumerate(((vel_held, vels_ref.at[1]), (state_held, out_ref))):
            copies.append(
                pltpu.make_async_copy(source.at[place], target.at[place], sems.at[1 + 2 * i + k])
            )
            copies[-1].start()
    for copy in copies:
        copy.wait()


def swap(x, axis, flip):
    return lax.ppermute(x, axis, [(i, i ^ flip) for i in range(lax.axis_size(axis))])


def spread(whole, rest, far):
    return dict(
        over=swap(far, "tp", 1),
        near=swap(whole, "tp", 1),
        rest_2=swap(rest, "tp", 2),
        rest_3=swap(rest, "tp", 3),
    )


def gather(own, got, far):
    return [own, got["near"], far, got["over"], got["rest_2"], got["rest_3"]]


def reduce(own, near, over, far, rest_2, rest_3):
    rest_2 = swap(rest_2, "tp", 2)
    rest_3 = swap(rest_3, "tp", 3)
    over = swap(over, "tp", 1)
    over, rest_2 = lax.optimization_barrier((over, rest_2))
    relayed = call(relay_body, shape(far.shape), [VMEM] * 2, VMEM, "relay")(far, over)
    relayed = swap(relayed, "tp", 2)
    near = swap(near, "tp", 1)
    return own, near, relayed, rest_2, rest_3


def pinned(x, space):
    return pltpu.with_memory_space_constraint(x, space)


def fast(latents, step_index, mod_table, base_up, base_down, up_a, up_b, down_a, down_b):
    tp, dp = lax.axis_size("tp"), lax.axis_size("dp")
    count, width = latents.shape
    rows = count * tp
    half = width // 2
    hidden = base_up.shape[1]
    rank = up_b.shape[0]
    both = 2 * rank * dp
    height = 2 * rank
    mods = jnp.transpose(mod_table, (1, 0, 2))
    spread_shapes = (shape((count, width)), shape((count, half)), shape((count, half)))

    sources = (up_a.T, down_b, up_b, down_a.T, step_index, latents, mods)
    p_own, q_own, normed, far, rest = call(
        functools.partial(prepare_body, dp, rank),
        (
            shape((height, up_a.shape[0] // height * both)),
            shape((height, hidden)),
        )
        + spread_shapes,
        [HBM] * 7,
        (VMEM,) * 5,
        "prepare",
        flops=16 * rows * width * hidden,
        scratch=[(pltpu.SMEM if a is step_index else pltpu.VMEM)(a.shape, a.dtype) for a in sources]
        + [pltpu.SemaphoreType.DMA((7,))],
    )(*[pinned(a, pltpu.HBM) for a in sources])

    far = swap(far, "tp", 2)
    p_line = jnp.concatenate([p_own] + [swap(p_own, "tp", k) for k in (1, 2, 3)], axis=1)
    p_line, q_own = lax.optimization_barrier((p_line, q_own))
    p_far = swap(p_line, "dp", 2)
    q_far = swap(q_own, "dp", 2)
    got = spread(normed, rest, far)
    keys = ("near", "rest_2", "rest_3", "over")
    p_far, q_far, held = lax.optimization_barrier((p_far, q_far, [got[k] for k in keys]))
    got.update(zip(keys, held))
    near = [swap(a, "dp", 1) for a in (p_line, q_own, p_far, q_far)]
    factors = call(
        functools.partial(assemble_body, tp, dp),
        (
            pltpu.VMEM((width, both), BF16),
            pltpu.VMEM((both, hidden), BF16),
            pltpu.VMEM((both, width), BF16),
            pltpu.VMEM((hidden, both), BF16),
        ),
        [VMEM] * (2 * dp),
        (VMEM,) * 4,
        "assemble_factors",
    )(p_line, near[0], p_far, near[2], q_own, near[1], q_far, near[3])
    resident = [pinned(a, pltpu.VMEM) for a in (*factors, base_up, base_down)]

    def block(parts):
        return call(
            functools.partial(block_body, rank),
            (
                shape((count, width), F32),
                shape((count, width)),
                shape((count, half)),
                shape((count, half), F32),
                shape((count, half)),
                shape((count, half)),
            ),
            [VMEM] * 12,
            (VMEM,) * 6,
            "block",
            [pltpu.VMEM((rows, width), BF16), pltpu.VMEM((rows, hidden), BF16)],
            flops=4 * rows * width * hidden,
            bytes_accessed=4 * width * hidden,
        )(*parts, *resident)

    sums = block(gather(normed, got, far))
    vel, state, normed, far, rest = call(
        middle_body,
        (shape((count, width), F32), shape((count, width), F32)) + spread_shapes,
        [SMEM] + [VMEM] * 7,
        (VMEM,) * 5,
        "first_update",
    )(step_index, latents, mods, *reduce(*sums))
    far = swap(far, "tp", 2)
    sums = block(gather(normed, spread(normed, rest, far), far))
    return call(
        last_body,
        (shape((2, count, width), F32), shape((count, width), F32)),
        [SMEM] + [VMEM] * 8,
        (HBM,) * 2,
        "second_update",
        [pltpu.VMEM((count, width), F32)] * 2 + [pltpu.SemaphoreType.DMA((5,))],
    )(step_index, mods, vel, state, *reduce(*sums))


def normalize(state, shift, scale):
    mean = jnp.mean(state, axis=1, keepdims=True)
    centered = state - mean
    spread = jnp.mean(centered * centered, axis=1, keepdims=True)
    return (centered * lax.rsqrt(spread + 1e-06) * (1.0 + scale) + shift).astype(jnp.bfloat16)


def plain(latents, step_index, mod_table, base_up, base_down, up_a, up_b, down_a, down_b):
    full_up_a, full_down_b = (
        lax.all_gather(up_a, ("dp", "tp"), axis=0, tiled=True),
        lax.all_gather(down_b, ("dp", "tp"), axis=1, tiled=True),
    )
    cols_up_b, rows_down_a = (
        lax.all_gather(up_b, "dp", axis=0, tiled=True),
        lax.all_gather(down_a, "dp", axis=1, tiled=True),
    )
    merged_up = (
        base_up.astype(jnp.float32)
        + jnp.dot(full_up_a, cols_up_b, preferred_element_type=jnp.float32)
    ).astype(jnp.bfloat16)
    merged_down = (
        base_down.astype(jnp.float32)
        + jnp.dot(rows_down_a, full_down_b, preferred_element_type=jnp.float32)
    ).astype(jnp.bfloat16)
    own_count = latents.shape[0]
    group_rows = own_count * lax.axis_size("tp")
    image_count = step_index.shape[0]
    image_rows = group_rows // image_count
    own_start = lax.axis_index("tp") * own_count
    step_size = -1.0 / NSTEPS

    def row_steps(count, offset):
        rows = jnp.arange(count, dtype=jnp.int32)
        image = rows // image_rows
        picks = (image[:, None] == jnp.arange(image_count, dtype=jnp.int32)[None, :]).astype(
            jnp.int32
        )
        return jnp.sum(picks * step_index[None, :], axis=1) + offset

    def modulation(steps):
        onehot = (steps[:, None] == jnp.arange(NSTEPS, dtype=jnp.int32)[None, :]).astype(
            jnp.float32
        )
        shift = jnp.dot(onehot, mod_table[:, 0, :], precision=lax.Precision.HIGHEST)
        scale = jnp.dot(onehot, mod_table[:, 1, :], precision=lax.Precision.HIGHEST)
        gate = jnp.dot(onehot, mod_table[:, 2, :], precision=lax.Precision.HIGHEST)
        return (shift, scale, gate)

    def project(normed):
        upper = jnp.dot(normed, merged_up, preferred_element_type=jnp.float32)
        hidden = jax.nn.gelu(upper, approximate=True).astype(jnp.bfloat16)
        return jnp.dot(hidden, merged_down, preferred_element_type=jnp.float32)

    state_all = lax.all_gather(latents, "tp", axis=0, tiled=True).astype(jnp.float32)
    shift, scale, gate = modulation(row_steps(group_rows, 0))
    normed = normalize(state_all, shift, scale)
    first = gate * lax.psum(project(normed), "tp")
    state_all = state_all + step_size * first
    shift, scale, gate = modulation(row_steps(group_rows, 1))
    normed = normalize(state_all, shift, scale)
    gate_own = lax.dynamic_slice_in_dim(gate, own_start, own_count, 0)
    second = gate_own * lax.psum_scatter(project(normed), "tp", scatter_dimension=0, tiled=True)
    state_own = lax.dynamic_slice_in_dim(state_all, own_start, own_count, 0) + step_size * second
    first_own = lax.dynamic_slice_in_dim(first, own_start, own_count, 0)
    return (jnp.stack([first_own, second]), state_own)


def solution(mesh):
    tp, dp = mesh.shape["tp"], mesh.shape["dp"]

    def local(*args):
        latents, step_index, mod_table, base_up, base_down, up_a, up_b = args[:7]
        whole_tiles = (
            tp == 4
            and dp == 4
            and latents.shape[0] == 2 * up_b.shape[0]
            and base_up.shape[1] % 256 == 0
            and base_up.shape[0] % 256 == 0
            and up_b.shape[0] % 16 == 0
            and up_a.shape[0] % (2 * up_b.shape[0]) == 0
            and tp % step_index.shape[0] == 0
        )
        return (fast if whole_tiles else plain)(*args)

    return jax.shard_map(
        local,
        mesh=mesh,
        in_specs=(
            P(("grp", "dp", "tp"), None),
            P(("grp", "dp")),
            P(),
            P(None, "tp"),
            P("tp", None),
            P(("dp", "tp"), None),
            P("dp", "tp"),
            P("tp", "dp"),
            P(None, ("dp", "tp")),
        ),
        out_specs=(P(None, ("grp", "dp", "tp"), None), P(("grp", "dp", "tp"), None)),
        check_vma=False,
    )
```

```python
import functools

import jax
import jax.numpy as jnp
from jax import lax
from jax.experimental import pallas as pl
from jax.experimental.pallas import tpu as pltpu
from jax.sharding import PartitionSpec as P

NSTEPS = 4
STEP_SIZE = -1.0 / NSTEPS
BF16, F32 = jnp.bfloat16, jnp.float32
VMEM_GRANT = 4 << 20
VMEM = pl.BlockSpec(memory_space=pltpu.VMEM)
SMEM = pl.BlockSpec(memory_space=pltpu.SMEM)
HBM = pl.BlockSpec(memory_space=pltpu.HBM)
NT = (((1,), (1,)), ((), ()))


def call(body, outs, in_specs, out_specs, name, scratch=(), flops=0, bytes_accessed=0):
    return pl.pallas_call(
        body,
        out_shape=outs,
        in_specs=in_specs,
        out_specs=out_specs,
        scratch_shapes=list(scratch),
        compiler_params=pltpu.CompilerParams(vmem_limit_bytes=VMEM_GRANT),
        cost_estimate=pl.CostEstimate(
            flops=flops, bytes_accessed=bytes_accessed, transcendentals=0
        ),
        name=name,
    )


def shape(dims, dtype=BF16):
    return jax.ShapeDtypeStruct(dims, dtype)


def modulated(state, shift, scale):
    mean = jnp.mean(state, axis=1, keepdims=True)
    centered = state - mean
    spread = jnp.mean(centered * centered, axis=1, keepdims=True)
    return (centered * lax.rsqrt(spread + 1e-06) * (1.0 + scale) + shift).astype(BF16)


def spread_out(normed, out_ref, far_ref, rest_ref):
    half = far_ref.shape[1]
    out_ref[...] = normed
    far_ref[...] = normed[:, :half]
    rest_ref[...] = normed[:, half:]


def gelu(x):
    return x * (0.5 * (1.0 + jnp.tanh(0.7978845608028654 * (x + 0.044715 * (x * x * x)))))


def own_image(images):
    tp = lax.axis_size("tp")
    return lax.axis_index("tp") * images // tp


def mod_row(mod_ref, which, step):
    return mod_ref[which, pl.ds(step, 1), :]


def prepare_body(slots, rank, *refs):
    sources, outs, held, sems = refs[:7], refs[7:12], refs[12:19], refs[-1]
    copies = [
        pltpu.make_async_copy(src, dst, sems.at[i])
        for i, (src, dst) in enumerate(zip(sources, held))
    ]
    for copy in copies:
        copy.start()
    for copy in copies:
        copy.wait()
    ua_ref, db_ref, ub_ref, da_ref, steps_ref, lat_ref, mod_ref = held
    p_ref, q_ref = outs[:2]
    rows = []
    for slot in range(slots):
        part = pl.ds(slot * rank, rank)
        rows += [ua_ref[part, :], db_ref[part, :]]
    both = jnp.concatenate(rows, axis=0)
    width = both.shape[0]
    eye = (
        lax.broadcasted_iota(jnp.int32, (width, width), 0)
        == lax.broadcasted_iota(jnp.int32, (width, width), 1)
    ).astype(F32)
    cols = lax.dot_general(
        both, eye.astype(BF16), (((0,), (0,)), ((), ())), preferred_element_type=F32
    ).astype(BF16)
    height = p_ref.shape[0]
    for piece in range(cols.shape[0] // height):
        p_ref[:, piece * width : (piece + 1) * width] = cols[piece * height : (piece + 1) * height, :]
    q_ref[0:rank, :] = ub_ref[...]
    q_ref[rank : 2 * rank, :] = da_ref[...]
    step = steps_ref[own_image(steps_ref.shape[0])]
    state = lat_ref[...].astype(F32)
    spread_out(modulated(state, mod_row(mod_ref, 0, step), mod_row(mod_ref, 1, step)), *outs[2:])


def assemble_body(tp, dp, *refs):
    p_parts, q_parts, (p_ref, q_ref, pt_ref, qt_ref) = refs[:dp], refs[dp : 2 * dp], refs[2 * dp :]
    me_tp, me_dp = lax.axis_index("tp"), lax.axis_index("dp")
    height = q_parts[0].shape[0]
    width = p_ref.shape[1]
    per_block = p_ref.shape[0] // (tp * dp)
    pieces = per_block // height
    for j in range(dp):
        owner = me_dp ^ j
        q_ref[pl.ds(pl.multiple_of(owner * height, height), height), :] = q_parts[j][...]
        for k in range(tp):
            base = (owner * tp + (me_tp ^ k)) * per_block
            for piece in range(pieces):
                col = (k * pieces + piece) * width
                p_ref[pl.ds(pl.multiple_of(base + piece * height, height), height), :] = p_parts[j][
                    :, col : col + width
                ]
    pt_ref[...] = p_ref[...].T
    qt_ref[...] = q_ref[...].T


def block_body(rank, *refs):
    x_refs, (p_ref, q_ref, pt_ref, qt_ref, wu_ref, wd_ref), refs = refs[:6], refs[6:12], refs[12:]
    outs, (x_all, hidden) = refs[:6], refs[6:]
    count, width = x_refs[0].shape
    half = width // 2
    own_ref, near_ref, far_ref, over_ref, rest_2_ref, rest_3_ref = x_refs
    x_all[:count, :] = own_ref[...]
    x_all[count : 2 * count, :] = near_ref[...]
    x_all[2 * count : 3 * count, :half] = far_ref[...]
    x_all[2 * count : 3 * count, half:] = rest_2_ref[...]
    x_all[3 * count :, :half] = over_ref[...]
    x_all[3 * count :, half:] = rest_3_ref[...]
    lanes = lax.broadcasted_iota(jnp.int32, (1, p_ref.shape[1]), 1)
    first_half = (lanes // rank) % 2 == 0
    low = jnp.dot(x_all[...], p_ref[...], preferred_element_type=F32)
    low = jnp.where(first_half, low, 0.0).astype(BF16)
    tile = hidden.shape[1] // 3

    def upper(i):
        cols = slice(i * tile, (i + 1) * tile)
        out = jnp.dot(x_all[...], wu_ref[:, cols], preferred_element_type=F32)
        return out + jnp.dot(low, q_ref[:, cols], preferred_element_type=F32)

    ahead = upper(0)
    for i in range(3):
        now = ahead
        if i < 2:
            ahead = upper(i + 1)
        hidden[:, i * tile : (i + 1) * tile] = gelu(now).astype(BF16)
    low = jnp.dot(hidden[...], qt_ref[...], preferred_element_type=F32)
    low = jnp.where(first_half, 0.0, low).astype(BF16)
    own_out, near_out, over_out, far_out, rest_2_out, rest_3_out = outs
    out = jnp.dot(hidden[...], wd_ref[...], preferred_element_type=F32)
    out += jnp.dot(low, pt_ref[...], preferred_element_type=F32)
    own_out[...] = out[:count]
    near_out[...] = out[count : 2 * count].astype(BF16)
    far_out[...] = out[2 * count : 3 * count, :half]
    over_out[...] = out[3 * count :, :half].astype(BF16)
    rest_2_out[...] = out[2 * count : 3 * count, half:].astype(BF16)
    rest_3_out[...] = out[3 * count :, half:].astype(BF16)


def relay_body(mine_ref, got_ref, out_ref):
    out_ref[...] = (mine_ref[...] + got_ref[...].astype(F32)).astype(BF16)


def summed(own_ref, near_ref, far_ref, rest_2_ref, rest_3_ref):
    half = far_ref.shape[1]
    total = own_ref[...] + near_ref[...].astype(F32)
    first = total[:, :half] + far_ref[...].astype(F32)
    second = total[:, half:] + rest_2_ref[...].astype(F32) + rest_3_ref[...].astype(F32)
    return first, second


def middle_body(steps_ref, lat_ref, mod_ref, *refs):
    parts, (vel_ref, state_ref, out_ref, far_ref, rest_ref) = refs[:5], refs[5:]
    step = steps_ref[own_image(steps_ref.shape[0])]
    vel = mod_row(mod_ref, 2, step) * jnp.concatenate(summed(*parts), axis=1)
    state = lat_ref[...].astype(F32) + STEP_SIZE * vel
    vel_ref[...] = vel
    state_ref[...] = state
    normed = modulated(state, mod_row(mod_ref, 0, step + 1), mod_row(mod_ref, 1, step + 1))
    spread_out(normed, out_ref, far_ref, rest_ref)


def last_body(steps_ref, mod_ref, vel_ref, state_ref, *refs):
    parts, (vels_ref, out_ref, vel_held, state_held, sems) = refs[:5], refs[5:]
    copies = [pltpu.make_async_copy(vel_ref, vels_ref.at[0], sems.at[0])]
    copies[0].start()
    step = steps_ref[own_image(steps_ref.shape[0])] + 1
    gate = mod_row(mod_ref, 2, step)
    half = state_ref.shape[1] // 2
    for i, total in enumerate(summed(*parts)):
        cols = slice(i * half, (i + 1) * half)
        vel = gate[:, cols] * total
        vel_held[:, cols] = vel
        state_held[:, cols] = state_ref[:, cols] + STEP_SIZE * vel
        place = (slice(None), pl.ds(i * half, half))
        for k, (source, target) in enumerate(((vel_held, vels_ref.at[1]), (state_held, out_ref))):
            copies.append(
                pltpu.make_async_copy(source.at[place], target.at[place], sems.at[1 + 2 * i + k])
            )
            copies[-1].start()
    for copy in copies:
        copy.wait()


def swap(x, axis, flip):
    return lax.ppermute(x, axis, [(i, i ^ flip) for i in range(lax.axis_size(axis))])


def spread(whole, rest, far):
    return dict(
        over=swap(far, "tp", 1),
        near=swap(whole, "tp", 1),
        rest_2=swap(rest, "tp", 2),
        rest_3=swap(rest, "tp", 3),
    )


def gather(own, got, far):
    return [own, got["near"], far, got["over"], got["rest_2"], got["rest_3"]]


def reduce(own, near, over, far, rest_2, rest_3):
    rest_2 = swap(rest_2, "tp", 2)
    rest_3 = swap(rest_3, "tp", 3)
    over = swap(over, "tp", 1)
    over, rest_2 = lax.optimization_barrier((over, rest_2))
    relayed = call(relay_body, shape(far.shape), [VMEM] * 2, VMEM, "relay")(far, over)
    relayed = swap(relayed, "tp", 2)
    near = swap(near, "tp", 1)
    return own, near, relayed, rest_2, rest_3


def pinned(x, space):
    return pltpu.with_memory_space_constraint(x, space)


def fast(latents, step_index, mod_table, base_up, base_down, up_a, up_b, down_a, down_b):
    tp, dp = lax.axis_size("tp"), lax.axis_size("dp")
    count, width = latents.shape
    rows = count * tp
    half = width // 2
    hidden = base_up.shape[1]
    rank = up_b.shape[0]
    both = 2 * rank * dp
    height = 2 * rank
    mods = jnp.transpose(mod_table, (1, 0, 2))
    spread_shapes = (shape((count, width)), shape((count, half)), shape((count, half)))

    sources = (up_a.T, down_b, up_b, down_a.T, step_index, latents, mods)
    p_own, q_own, normed, far, rest = call(
        functools.partial(prepare_body, dp, rank),
        (
            shape((height, up_a.shape[0] // height * both)),
            shape((height, hidden)),
        )
        + spread_shapes,
        [HBM] * 7,
        (VMEM,) * 5,
        "prepare",
        flops=16 * rows * width * hidden,
        scratch=[(pltpu.SMEM if a is step_index else pltpu.VMEM)(a.shape, a.dtype) for a in sources]
        + [pltpu.SemaphoreType.DMA((7,))],
    )(*[pinned(a, pltpu.HBM) for a in sources])

    far = swap(far, "tp", 2)
    p_line = jnp.concatenate([p_own] + [swap(p_own, "tp", k) for k in (1, 2, 3)], axis=1)
    p_line, q_own = lax.optimization_barrier((p_line, q_own))
    p_far = swap(p_line, "dp", 2)
    q_far = swap(q_own, "dp", 2)
    got = spread(normed, rest, far)
    keys = ("near", "rest_2", "rest_3", "over")
    p_far, q_far, held = lax.optimization_barrier((p_far, q_far, [got[k] for k in keys]))
    got.update(zip(keys, held))
    near = [swap(a, "dp", 1) for a in (p_line, q_own, p_far, q_far)]
    factors = call(
        functools.partial(assemble_body, tp, dp),
        (
            pltpu.VMEM((width, both), BF16),
            pltpu.VMEM((both, hidden), BF16),
            pltpu.VMEM((both, width), BF16),
            pltpu.VMEM((hidden, both), BF16),
        ),
        [VMEM] * (2 * dp),
        (VMEM,) * 4,
        "assemble_factors",
    )(p_line, near[0], p_far, near[2], q_own, near[1], q_far, near[3])
    resident = [pinned(a, pltpu.VMEM) for a in (*factors, base_up, base_down)]

    def block(parts):
        return call(
            functools.partial(block_body, rank),
            (
                shape((count, width), F32),
                shape((count, width)),
                shape((count, half)),
                shape((count, half), F32),
                shape((count, half)),
                shape((count, half)),
            ),
            [VMEM] * 12,
            (VMEM,) * 6,
            "block",
            [pltpu.VMEM((rows, width), BF16), pltpu.VMEM((rows, hidden), BF16)],
            flops=4 * rows * width * hidden,
            bytes_accessed=4 * width * hidden,
        )(*parts, *resident)

    sums = block(gather(normed, got, far))
    vel, state, normed, far, rest = call(
        middle_body,
        (shape((count, width), F32), shape((count, width), F32)) + spread_shapes,
        [SMEM] + [VMEM] * 7,
        (VMEM,) * 5,
        "first_update",
    )(step_index, latents, mods, *reduce(*sums))
    far = swap(far, "tp", 2)
    sums = block(gather(normed, spread(normed, rest, far), far))
    return call(
        last_body,
        (shape((2, count, width), F32), shape((count, width), F32)),
        [SMEM] + [VMEM] * 8,
        (HBM,) * 2,
        "second_update",
        [pltpu.VMEM((count, width), F32)] * 2 + [pltpu.SemaphoreType.DMA((5,))],
    )(step_index, mods, vel, state, *reduce(*sums))


def normalize(state, shift, scale):
    mean = jnp.mean(state, axis=1, keepdims=True)
    centered = state - mean
    spread = jnp.mean(centered * centered, axis=1, keepdims=True)
    return (centered * lax.rsqrt(spread + 1e-06) * (1.0 + scale) + shift).astype(jnp.bfloat16)


def plain(latents, step_index, mod_table, base_up, base_down, up_a, up_b, down_a, down_b):
    full_up_a, full_down_b = (
        lax.all_gather(up_a, ("dp", "tp"), axis=0, tiled=True),
        lax.all_gather(down_b, ("dp", "tp"), axis=1, tiled=True),
    )
    cols_up_b, rows_down_a = (
        lax.all_gather(up_b, "dp", axis=0, tiled=True),
        lax.all_gather(down_a, "dp", axis=1, tiled=True),
    )
    merged_up = (
        base_up.astype(jnp.float32)
        + jnp.dot(full_up_a, cols_up_b, preferred_element_type=jnp.float32)
    ).astype(jnp.bfloat16)
    merged_down = (
        base_down.astype(jnp.float32)
        + jnp.dot(rows_down_a, full_down_b, preferred_element_type=jnp.float32)
    ).astype(jnp.bfloat16)
    own_count = latents.shape[0]
    group_rows = own_count * lax.axis_size("tp")
    image_count = step_index.shape[0]
    image_rows = group_rows // image_count
    own_start = lax.axis_index("tp") * own_count
    step_size = -1.0 / NSTEPS

    def row_steps(count, offset):
        rows = jnp.arange(count, dtype=jnp.int32)
        image = rows // image_rows
        picks = (image[:, None] == jnp.arange(image_count, dtype=jnp.int32)[None, :]).astype(
            jnp.int32
        )
        return jnp.sum(picks * step_index[None, :], axis=1) + offset

    def modulation(steps):
        onehot = (steps[:, None] == jnp.arange(NSTEPS, dtype=jnp.int32)[None, :]).astype(
            jnp.float32
        )
        shift = jnp.dot(onehot, mod_table[:, 0, :], precision=lax.Precision.HIGHEST)
        scale = jnp.dot(onehot, mod_table[:, 1, :], precision=lax.Precision.HIGHEST)
        gate = jnp.dot(onehot, mod_table[:, 2, :], precision=lax.Precision.HIGHEST)
        return (shift, scale, gate)

    def project(normed):
        upper = jnp.dot(normed, merged_up, preferred_element_type=jnp.float32)
        hidden = jax.nn.gelu(upper, approximate=True).astype(jnp.bfloat16)
        return jnp.dot(hidden, merged_down, preferred_element_type=jnp.float32)

    state_all = lax.all_gather(latents, "tp", axis=0, tiled=True).astype(jnp.float32)
    shift, scale, gate = modulation(row_steps(group_rows, 0))
    normed = normalize(state_all, shift, scale)
    first = gate * lax.psum(project(normed), "tp")
    state_all = state_all + step_size * first
    shift, scale, gate = modulation(row_steps(group_rows, 1))
    normed = normalize(state_all, shift, scale)
    gate_own = lax.dynamic_slice_in_dim(gate, own_start, own_count, 0)
    second = gate_own * lax.psum_scatter(project(normed), "tp", scatter_dimension=0, tiled=True)
    state_own = lax.dynamic_slice_in_dim(state_all, own_start, own_count, 0) + step_size * second
    first_own = lax.dynamic_slice_in_dim(first, own_start, own_count, 0)
    return (jnp.stack([first_own, second]), state_own)


def solution(mesh):
    tp, dp = mesh.shape["tp"], mesh.shape["dp"]

    def local(*args):
        latents, step_index, mod_table, base_up, base_down, up_a, up_b = args[:7]
        whole_tiles = (
            tp == 4
            and dp == 4
            and latents.shape[0] == 2 * up_b.shape[0]
            and base_up.shape[1] % 256 == 0
            and base_up.shape[0] % 256 == 0
            and up_b.shape[0] % 16 == 0
            and up_a.shape[0] % (2 * up_b.shape[0]) == 0
            and tp % step_index.shape[0] == 0
        )
        return (fast if whole_tiles else plain)(*args)

    return jax.shard_map(
        local,
        mesh=mesh,
        in_specs=(
            P(("grp", "dp", "tp"), None),
            P(("grp", "dp")),
            P(),
            P(None, "tp"),
            P("tp", None),
            P(("dp", "tp"), None),
            P("dp", "tp"),
            P("tp", "dp"),
            P(None, ("dp", "tp")),
        ),
        out_specs=(P(None, ("grp", "dp", "tp"), None), P(("grp", "dp", "tp"), None)),
        check_vma=False,
    )
```
